512 devices in a mesh: node: 32 (over x, z), feat: 16 (over y, core).
Axes of the slice: x: 4, y: 8, z: 8, core: 2. Of those that a mesh axis runs over, the one named last changes fastest.
Arguments:
- x_far: bfloat16 [128, 524288], P('feat', 'node'), may hold values from -6 to 6
- x_near: bfloat16 [128, 65536], P('feat', 'node'), may hold values from -6 to 6
- tile_src: int32 [32768], P('node'), may hold values from 0 to 127
- tile_dst: int32 [32768], P('node'), may hold values from 0 to 15
- tile_rows: int32 [32768], P('node'), may hold values from 0 to 128, as said below
- tile_cols: int32 [32768, 4, 128], P('node'), may hold values from 0 to 127
- seed_nbrs: int32 [4096, 10], P('node'), may hold values from 0 to 2047
- labels: int32 [4096], P('node'), may hold values from 0 to 171
- self_one: bfloat16 [256, 128], P(None, 'feat'), may hold values from -0.5 to 0.5
- neigh_one: bfloat16 [256, 128], P(None, 'feat'), may hold values from -0.5 to 0.5
- self_two: bfloat16 [172, 256], P(None, 'feat'), may hold values from -0.375 to 0.375
- neigh_two: bfloat16 [172, 256], P(None, 'feat'), may hold values from -0.375 to 0.375
Outputs:
- logits: float32 [172, 4096], P(None, 'node')
- loss: float32 [4096], P('node')
The draws below stay inside these ranges and needn't reach their ends.
Inputs may be any that keep to these rules, and one draw needn't show every extreme that they name: `tile_rows`: slots j with (j mod 32) < a count are used; for some target devices every source device fills all 32 slots; slot 0 of every source and target pair holds 128 rows.
All inputs are finite; a program needn't handle non-finite values.
Results may differ from the reference program's by a relative error of at most 0.003.
Values may be sent and summed in bfloat16 or wider, within the bound.
A program may use at most 64 MiB of HBM per device.

```python
import jax
import jax.numpy as jnp
from jax import lax

F = 128
H = 256
C = 172
K = 4
FAN2 = 10
CAP = 32
N1_DEV = 2048
N2_DEV = 16384
S_DEV = 128
TILE_DEV = 1024
TILES = 32768
N1 = 65536
N2 = 524288
SEEDS = 4096
N_NODE = 32


def draw_tile_rows(key, part):
    key = jax.random.fold_in(key, 11)
    first, second, third, fourth = jax.random.split(key, 4)
    busy = jax.random.randint(first, (N_NODE,), 0, 4) == 0
    busy = busy | (jnp.arange(N_NODE) == jax.random.randint(second, (), 0, N_NODE))
    used = jnp.where(busy[None, :], CAP, jax.random.randint(third, (N_NODE, N_NODE), 1, CAP // 2 + 1))
    slots = jnp.arange(CAP)
    live = slots[None, None, :] < used[:, :, None]
    rows = jax.random.randint(fourth, (N_NODE, N_NODE, CAP), 1, 129)
    rows = jnp.where(slots[None, None, :] == 0, 128, rows)
    return jnp.where(live, rows, 0).reshape(TILES).astype(jnp.int32)


def touch_ends(array, own_key, least, largest):
    longest = array.shape.index(max(array.shape))
    spots = []
    for shift in (0, 1):
        where = [jax.random.randint(jax.random.fold_in(own_key, axis), (), 0, length) for axis, length in enumerate(array.shape)]
        where[longest] = (where[longest] + shift) % array.shape[longest]
        spots.append(tuple(where))
    return array.at[spots[0]].set(least).at[spots[1]].set(largest)


def levels(rng, extent, cuts, smallest, high):
    gain, own = 1.0, jax.random.fold_in(rng, 6)
    for dim, blocks in cuts:
        heights = jnp.exp(jax.random.uniform(jax.random.fold_in(own, dim), (blocks,), jnp.float32, smallest / len(cuts), high / len(cuts)))
        gain = gain * jnp.repeat(heights, extent[dim] // blocks).reshape([-1 if axis == dim else 1 for axis in range(len(extent))])
    return gain


def normal_values(key, shape, spread, limit, cuts=(), kind=jnp.bfloat16):
    entries = spread * jax.random.normal(key, shape, jnp.float32)
    if cuts:
        entries = entries * levels(key, shape, cuts, -0.22, 0.18)
    return jnp.clip(entries, -limit, limit).astype(kind)


def setup_inputs(seed: int = 0) -> dict:
    streams_of = jax.random.split(jax.random.key(seed), 13)
    x_far = normal_values(streams_of[0], (F, N2), 1.0, 6.0, ((0, 16), (1, 32)))
    x_near = normal_values(streams_of[1], (F, N1), 1.0, 6.0, ((0, 16), (1, 32)))
    tile_src = touch_ends(jax.random.randint(streams_of[2], (TILES,), 0, N2_DEV // 128), jax.random.fold_in(streams_of[2], 1), 0, (N2_DEV // 128) - 1).astype(jnp.int32)
    tile_dst = touch_ends(jax.random.randint(streams_of[3], (TILES,), 0, N1_DEV // 128), jax.random.fold_in(streams_of[3], 1), 0, (N1_DEV // 128) - 1).astype(jnp.int32)
    tile_rows = draw_tile_rows(jax.random.fold_in(streams_of[12], 71), 0)
    tile_cols = touch_ends(jax.random.randint(streams_of[5], (TILES, K, 128), 0, 128), jax.random.fold_in(streams_of[5], 1), 0, 127).astype(jnp.int32)
    seed_nbrs = touch_ends(jax.random.randint(streams_of[6], (SEEDS, FAN2), 0, N1_DEV), jax.random.fold_in(streams_of[6], 1), 0, N1_DEV - 1).astype(jnp.int32)
    labels = touch_ends(jax.random.randint(streams_of[7], (SEEDS,), 0, C), jax.random.fold_in(streams_of[7], 1), 0, C - 1).astype(jnp.int32)
    self_one = normal_values(streams_of[8], (H, F), F ** -0.5, 0.5, ((1, 16),))
    neigh_one = normal_values(streams_of[9], (H, F), F ** -0.5, 0.5, ((1, 16),))
    self_two = normal_values(streams_of[10], (C, H), H ** -0.5, 0.375, ((1, 16),))
    neigh_two = normal_values(streams_of[11], (C, H), H ** -0.5, 0.375, ((1, 16),))
    return {"x_far": x_far, "x_near": x_near, "tile_src": tile_src, "tile_dst": tile_dst, "tile_rows": tile_rows, "tile_cols": tile_cols, "seed_nbrs": seed_nbrs, "labels": labels, "self_one": self_one, "neigh_one": neigh_one, "self_two": self_two, "neigh_two": neigh_two}


def tile_counts(cols, rows):
    lanes = jnp.arange(128, dtype=jnp.int32)
    live = (lanes[None, :] < rows[:, None]).astype(jnp.float32)
    hits = jnp.sum((cols[..., None] == lanes).astype(jnp.float32), axis=1)
    return hits * live[:, :, None], live


def reference(x_far, x_near, tile_src, tile_dst, tile_rows, tile_cols, seed_nbrs, labels, self_one, neigh_one, self_two, neigh_two):
    nb1 = N1_DEV // 128
    nb2 = N2_DEV // 128
    blocks = x_far.astype(jnp.float32).reshape(F, N_NODE * nb2, 128)

    def device_step(carry, items):
        agg, deg = carry
        index, srcs, dsts, rows, cols = items
        glob_src = index * nb2 + srcs

        def group(parts):
            src_g, cols_g, rows_g = parts
            counts, live = tile_counts(cols_g, rows_g)
            chosen = jnp.take(blocks, src_g, axis=1)
            return jnp.einsum("fgc,grc->gfr", chosen, counts), live

        partial_value, live = lax.map(group, (glob_src.reshape(N_NODE, CAP), cols.reshape(N_NODE, CAP, K, 128), rows.reshape(N_NODE, CAP)))
        target = (jnp.arange(N_NODE, dtype=jnp.int32)[:, None] * nb1 + dsts.reshape(N_NODE, CAP)).reshape(-1)
        agg = agg + jax.ops.segment_sum(partial_value.reshape(TILE_DEV, F, 128), target, N_NODE * nb1)
        deg = deg + jax.ops.segment_sum(K * live.reshape(TILE_DEV, 128), target, N_NODE * nb1)
        return (agg, deg), None

    start = (jnp.zeros((N_NODE * nb1, F, 128), jnp.float32), jnp.zeros((N_NODE * nb1, 128), jnp.float32))
    items = (jnp.arange(N_NODE, dtype=jnp.int32), tile_src.reshape(N_NODE, TILE_DEV), tile_dst.reshape(N_NODE, TILE_DEV), tile_rows.reshape(N_NODE, TILE_DEV), tile_cols.reshape(N_NODE, TILE_DEV, K, 128))
    (agg, deg), _ = lax.scan(device_step, start, items)
    agg = agg.transpose(1, 0, 2).reshape(F, N1)
    deg = deg.reshape(N1)
    mean_one = (agg / jnp.maximum(deg, 1.0)[None, :]).astype(jnp.bfloat16)
    z = jnp.dot(self_one, x_near, preferred_element_type=jnp.float32) + jnp.dot(neigh_one, mean_one, preferred_element_type=jnp.float32)
    h = jnp.maximum(z, 0.0).astype(jnp.bfloat16)
    per_dev = h.reshape(H, N_NODE, N1_DEV).transpose(1, 0, 2)
    nbrs = seed_nbrs.reshape(N_NODE, S_DEV, FAN2)

    def seed_mean(parts):
        hidden, near = parts
        nodes = jnp.arange(N1_DEV, dtype=jnp.int32)
        counts = jnp.sum((nodes[:, None, None] == near[None]).astype(jnp.float32), axis=2)
        return jnp.dot(hidden.astype(jnp.float32), counts) / FAN2

    mean_two = lax.map(seed_mean, (per_dev, nbrs))
    mean_two = mean_two.transpose(1, 0, 2).reshape(H, SEEDS).astype(jnp.bfloat16)
    h_seed = per_dev[:, :, :S_DEV].transpose(1, 0, 2).reshape(H, SEEDS)
    logits = jnp.dot(self_two, h_seed, preferred_element_type=jnp.float32) + jnp.dot(neigh_two, mean_two, preferred_element_type=jnp.float32)
    classes = jnp.arange(C, dtype=jnp.int32)
    total = jnp.log(jnp.sum(jnp.exp(logits), axis=0))
    picked = jnp.sum(jnp.where(classes[:, None] == labels[None, :], logits, 0.0), axis=0)
    return logits, total - picked
```

```python
import functools

import jax
import jax.numpy as jnp
from jax import lax
from jax.experimental import pallas as pl
from jax.experimental.pallas import tpu as pltpu
from jax.sharding import PartitionSpec as P

FAN2 = 10
NX, NZ = 4, 8
LANES = 128
CHUNK = 8
MESH = pl.DeviceIdType.MESH
F32, BF16 = jnp.float32, jnp.bfloat16


def tiles_kernel(src, dst, rows, x_ref, cols_ref, out_ref, deg_ref, xs, *accs):
    per_step = out_ref.shape[0]
    step = pl.program_id(0)
    feat = lax.axis_index("feat")
    slots = cols_ref.shape[0] // per_step
    depth = cols_ref.shape[1]

    @pl.when(step == 0)
    def _():
        for b in range(xs.shape[0]):
            xs[b] = x_ref[:, b * LANES : (b + 1) * LANES].astype(F32)

    lane = lax.broadcasted_iota(jnp.int32, (8, LANES), 1)

    def target(j, _):
        for acc in accs:
            acc[...] = jnp.zeros_like(acc)
        deg = jnp.zeros((8, LANES), F32)
        for c in range(slots // CHUNK):
            base = (step * per_step + j) * slots + c * CHUNK
            valid = [rows[base + i] for i in range(CHUNK)]

            def work(deg):
                sums = []
                for i in range(CHUNK):
                    block = xs[src[base + i]]
                    t = j * slots + c * CHUNK + i
                    total = None
                    for k in range(depth):
                        index = jnp.broadcast_to(cols_ref[t, pl.ds(k, 1), :], (8, LANES))
                        got = jnp.take_along_axis(block, index, axis=1, mode="promise_in_bounds")
                        total = got if total is None else total + got
                    sums.append(jnp.where(lane < valid[i], total, 0.0))
                for i in range(CHUNK):
                    acc, d = accs[i % len(accs)], dst[base + i]
                    acc[d] += sums[i]
                    deg += jnp.where(lane < jnp.where(d == feat, valid[i], 0), 1.0, 0.0)
                return deg

            deg = lax.cond(functools.reduce(lambda a, b: a + b, valid) > 0, work, lambda d: d, deg)
        total = accs[0][...]
        for acc in accs[1:]:
            total += acc[...]
        out_ref[j] = total.reshape(out_ref.shape[1:]).astype(out_ref.dtype)
        deg_ref[0, pl.ds((step * per_step + j) % NZ, 1), :] = deg[0:1]
        return 0

    lax.fori_loop(0, per_step, target, 0)


def tile_sums(src, dst, rows, x, cols, near_blocks):
    nodes = NX * NZ
    smem = pl.BlockSpec(memory_space=pltpu.SMEM)
    return pl.pallas_call(
        tiles_kernel,
        grid=(NX,),
        out_shape=(
            jax.ShapeDtypeStruct((nodes, near_blocks * 8, LANES), BF16),
            jax.ShapeDtypeStruct((NX, NZ, LANES), F32),
        ),
        in_specs=[
            smem,
            smem,
            smem,
            pl.BlockSpec(x.shape, lambda e: (0, 0)),
            pl.BlockSpec((cols.shape[0] // NX, *cols.shape[1:]), lambda e: (e, 0, 0)),
        ],
        out_specs=(
            pl.BlockSpec((NZ, near_blocks * 8, LANES), lambda e: (e, 0, 0)),
            pl.BlockSpec((1, NZ, LANES), lambda e: (e, 0, 0)),
        ),
        scratch_shapes=[pltpu.VMEM((x.shape[1] // LANES, 8, LANES), F32)]
        + [pltpu.VMEM((near_blocks, 8, LANES), F32)] * 2,
    )(src, dst, rows, x, cols)


def exchange_kernel(
    parts, degp, xnear, weights, nbrs, out,
    wall, a1, b1, a2, b2, ac, ao, bo, bc, dgot, zs, zr, degs, s2, r2, s3, hs, r3, rh, s4, r4,
    wsem, xsend, xrecv, dsend, drecv, zsend, zrecv, fsem,
):
    node, f = lax.axis_index("node"), lax.axis_index("feat")
    x, z = node // NZ, node % NZ
    nf = wall.shape[0]
    xp, xm, xo = (x + 1) % NX, (x + NX - 1) % NX, (x + 2) % NX
    half = a1.shape[1]
    body = 2 * half

    def at(xx=x, zz=z, ff=f):
        return {"node": xx * NZ + zz, "feat": ff}

    def send(source, target, send_sem, recv_sem, device):
        copy = pltpu.make_async_remote_copy(
            src_ref=source, dst_ref=target, send_sem=send_sem, recv_sem=recv_sem,
            device_id=device, device_id_type=MESH,
        )
        copy.start()

    def landed(ref, sem):
        pltpu.make_async_copy(ref, ref, sem).wait()

    def order(i):
        return (4 + (1 - 2 * (i % 2)) * ((i + 1) // 2)) % NZ

    def loop(n, fn):
        lax.fori_loop(0, n, lambda i, c: (fn(i), c)[1], 0)

    barrier = pltpu.get_barrier_semaphore()

    def greet(device):
        pl.semaphore_signal(barrier, inc=1, device_id=device, device_id_type=MESH)

    loop(NX - 1, lambda i: greet(at(xx=(x + 1 + i) % NX)))
    loop(NZ - 1, lambda i: greet(at(zz=(z + 1 + i) % NZ)))
    loop(nf - 1, lambda i: greet(at(ff=(f + 1 + i) % nf)))
    pl.semaphore_wait(barrier, NX - 1 + NZ - 1 + nf - 1)

    def first(i):
        zi = (z + order(i)) % NZ
        send(parts.at[xo, zi, pl.ds(0, half)], a1.at[zi], xsend.at[0, zi], xrecv.at[0, zi], at(xx=xp))
        send(parts.at[xo, zi, pl.ds(half, half)], b1.at[zi], xsend.at[1, zi], xrecv.at[1, zi], at(xx=xm))

    loop(NZ, first)

    def degrees(i):
        xx = (x + 1 + i) % NX
        send(degp.at[xx], dgot.at[i], dsend.at[i], drecv.at[i], at(xx=xx))

    loop(NX - 1, degrees)

    def direct(i):
        zi = (z + order(i)) % NZ
        send(parts.at[xp, zi, pl.ds(half, half)], bo.at[zi], xsend.at[2, zi], xrecv.at[2, zi], at(xx=xp))
        send(parts.at[xm, zi, pl.ds(0, half)], ao.at[zi], xsend.at[3, zi], xrecv.at[3, zi], at(xx=xm))

    loop(NZ, direct)

    wall[f] = weights[...]
    loop(
        nf - 1,
        lambda i: send(weights, wall.at[f], wsem.at[0], wsem.at[1], at(ff=(f + 1 + i) % nf)),
    )

    def relay(i):
        zi = (z + order(i)) % NZ
        landed(a1.at[zi], xrecv.at[0, zi])
        a2[zi] = (a1[zi].astype(F32) + parts[xp, zi, pl.ds(0, half), :].astype(F32)).astype(BF16)
        send(a2.at[zi], ac.at[zi], xsend.at[4, zi], xrecv.at[4, zi], at(xx=xp))
        landed(b1.at[zi], xrecv.at[1, zi])
        b2[zi] = (b1[zi].astype(F32) + parts[xm, zi, pl.ds(half, half), :].astype(F32)).astype(BF16)
        send(b2.at[zi], bc.at[zi], xsend.at[5, zi], xrecv.at[5, zi], at(xx=xm))

    loop(NZ, relay)

    near = nbrs[...]
    columns = lax.broadcasted_iota(jnp.int32, (near.shape[0], LANES), 1) + f * LANES
    counts = jnp.zeros((near.shape[0], LANES), F32)
    for n in range(FAN2):
        counts += jnp.where(near[:, n : n + 1] == columns, 1.0, 0.0)
    counts = counts.astype(BF16)
    for b in range(nf):
        s2[b, 0:8] = xnear[:, b * LANES : (b + 1) * LANES].astype(F32)

    for i in range(NX - 1):
        landed(dgot.at[i], drecv.at[i])
    deg_x = degp[x] + dgot[0] + dgot[1] + dgot[2]
    deg_tile = jnp.concatenate([deg_x, jnp.zeros_like(deg_x)], axis=0).astype(BF16)

    def onward(i):
        dz = order(i)
        zi = (z + dz) % NZ
        for kind, ref in ((2, bo), (3, ao), (4, ac), (5, bc)):
            landed(ref.at[zi], xrecv.at[kind, zi])
        zs[zi, 0:half] = (
            parts[x, zi, pl.ds(0, half), :].astype(F32) + ao[zi].astype(F32) + ac[zi].astype(F32)
        ).astype(BF16)
        zs[zi, half:body] = (
            parts[x, zi, pl.ds(half, half), :].astype(F32) + bo[zi].astype(F32) + bc[zi].astype(F32)
        ).astype(BF16)
        zs[zi, body : body + 16] = deg_tile

        @pl.when(dz != 0)
        def _():
            send(zs.at[zi], zr.at[dz - 1], zsend.at[dz - 1], zrecv.at[dz - 1], at(zz=zi))

    loop(NZ, onward)

    own = zs[z]
    agg = own[0:body].astype(F32)
    deg = own[body : body + 16].astype(F32)
    for i in (3, 2, 4, 1, 5, 0, 6):
        landed(zr.at[i], zrecv.at[i])
        got = zr[i]
        agg += got[0:body].astype(F32)
        deg += got[body : body + 16].astype(F32)
    degs[...] = deg
    for b in range(nf):
        s2[b, 8:16] = agg[b * 8 : b * 8 + 8]

    r2[f] = s2[f]

    def spread(i):
        p = (f + 1 + i) % nf
        send(s2.at[p], r2.at[f], fsem.at[0], fsem.at[1], at(ff=p))

    loop(nf - 1, spread)
    scale = 1.0 / jnp.maximum(4.0 * degs[pl.ds(z, 1), :], 1.0)
    landed(r2.at[pl.ds(0, nf - 1)], fsem.at[1])
    both = r2[...].reshape(nf * 16, LANES)
    is_sum = lax.broadcasted_iota(jnp.int32, both.shape, 0) % 16 >= 8
    both = jnp.where(is_sum, both * scale, both).astype(BF16)
    landed(wall.at[pl.ds(0, nf - 1)], wsem.at[1])
    w1 = wall[:, 0:16, :].reshape(nf * 16, wall.shape[2])
    pre = lax.dot_general(both, w1, (((0,), (0,)), ((), ())), preferred_element_type=F32)
    hidden = jnp.maximum(pre, 0.0).astype(BF16)
    s3[...] = jnp.dot(counts, hidden, preferred_element_type=F32)

    @pl.when(f == 0)
    def _():
        hs[...] = hidden.astype(F32)

    def seeds_out(i):
        p = (f + 1 + i) % nf
        send(s3.at[pl.ds(p * 8, 8)], r3.at[f], fsem.at[2], fsem.at[3], at(ff=p))

        @pl.when(f == 0)
        def _():
            send(hs.at[pl.ds(p * 8, 8)], rh, fsem.at[4], fsem.at[5], at(ff=p))

    loop(nf - 1, seeds_out)
    r3[f] = s3[pl.ds(f * 8, 8), :]
    landed(r3.at[pl.ds(0, nf - 1)], fsem.at[3])
    mean = jnp.zeros(r3.shape[1:], F32)
    for p in range(nf):
        mean += r3[p]
    mean = (mean / FAN2).astype(BF16)

    @pl.when(f == 0)
    def _():
        rh[...] = hs[0:8, :]

    @pl.when(f != 0)
    def _():
        landed(rh, fsem.at[5])

    w2s = wall[:, 16:32, :].reshape(nf * 16, wall.shape[2])
    w2n = wall[:, 32:48, :].reshape(nf * 16, wall.shape[2])
    logits = jnp.dot(rh[...].astype(BF16), w2s, preferred_element_type=F32) + jnp.dot(
        mean, w2n, preferred_element_type=F32
    )
    s4[...] = logits
    r4[f] = logits
    loop(nf - 1, lambda i: send(s4, r4.at[f], fsem.at[6], fsem.at[7], at(ff=(f + 1 + i) % nf)))

    def sent(i):
        for kind, ref in ((0, a1), (1, b1), (2, bo), (3, ao), (4, ac), (5, bc)):
            landed(ref.at[i], xsend.at[kind, i])

    loop(NZ, sent)
    for i in range(NX - 1):
        landed(dgot.at[i], dsend.at[i])
    for i in range(NZ - 1):
        landed(zr.at[i], zsend.at[i])
    landed(wall.at[pl.ds(0, nf - 1)], wsem.at[0])
    landed(r2.at[pl.ds(0, nf - 1)], fsem.at[0])
    landed(r3.at[pl.ds(0, nf - 1)], fsem.at[2])

    @pl.when(f == 0)
    def _():
        landed(hs.at[pl.ds(0, 8 * (nf - 1))], fsem.at[4])

    landed(r4.at[pl.ds(0, nf - 1)], fsem.at[7])
    out[...] = r4[...]
    landed(r4.at[pl.ds(0, nf - 1)], fsem.at[6])


def exchange(parts, degp, xnear, weights, nbrs, feats, seeds):
    hid = weights.shape[1]
    rows = parts.shape[2]
    half = rows // 2
    vm = pl.BlockSpec(memory_space=pltpu.VMEM)
    quarter = pltpu.VMEM((NZ, half, LANES), BF16)
    dma = pltpu.SemaphoreType.DMA
    return pl.pallas_call(
        exchange_kernel,
        out_shape=jax.ShapeDtypeStruct((feats, 8, hid), F32),
        in_specs=[vm] * 5,
        out_specs=vm,
        scratch_shapes=[
            pltpu.VMEM((feats, *weights.shape), BF16),
            *[quarter] * 8,
            pltpu.VMEM((NX - 1, NZ, LANES), F32),
            pltpu.VMEM((NZ, rows + 16, LANES), BF16),
            pltpu.VMEM((NZ - 1, rows + 16, LANES), BF16),
            pltpu.VMEM((16, LANES), F32),
            pltpu.VMEM((feats, 16, LANES), F32),
            pltpu.VMEM((feats, 16, LANES), F32),
            pltpu.VMEM((seeds, hid), F32),
            pltpu.VMEM((LANES, hid), F32),
            pltpu.VMEM((feats, 8, hid), F32),
            pltpu.VMEM((8, hid), F32),
            pltpu.VMEM((8, hid), F32),
            pltpu.VMEM((feats, 8, hid), F32),
            dma((2,)),
            dma((6, NZ)),
            dma((6, NZ)),
            dma((NX - 1,)),
            dma((NX - 1,)),
            dma((NZ - 1,)),
            dma((NZ - 1,)),
            dma((8,)),
        ],
        compiler_params=pltpu.CompilerParams(
            collective_id=0, has_side_effects=True, vmem_limit_bytes=32 * 1024 * 1024
        ),
    )(parts, degp, xnear, weights, nbrs)


def loss_kernel(table, labels, logits, loss):
    full = jnp.transpose(table[...])
    rows = full[0 : logits.shape[0]]
    logits[...] = rows
    classes = lax.broadcasted_iota(jnp.int32, rows.shape, 0)
    picked = jnp.sum(jnp.where(classes == labels[...], rows, 0.0), axis=0, keepdims=True)
    loss[...] = jnp.log(jnp.sum(jnp.exp(rows), axis=0, keepdims=True)) - picked


def per_device(
    x_far,
    x_near,
    tile_src,
    tile_dst,
    tile_rows,
    tile_cols,
    seed_nbrs,
    labels,
    self_one,
    neigh_one,
    self_two,
    neigh_two,
):
    feats = lax.axis_size("feat")
    hid = self_one.shape[0]
    classes = self_two.shape[0]
    seeds = labels.shape[0]
    near_blocks = x_near.shape[1] // LANES
    pad = ((0, 0), (0, hid - classes))
    weights = jnp.concatenate(
        [self_one.T, neigh_one.T, jnp.pad(self_two.T, pad), jnp.pad(neigh_two.T, pad)], axis=0
    )
    parts, degp = tile_sums(tile_src, tile_dst, tile_rows, x_far, tile_cols, near_blocks)
    parts = parts.reshape(NX, NZ, near_blocks * 8, LANES)
    table = exchange(parts, degp, x_near, weights, seed_nbrs, feats, seeds)
    logits, loss = pl.pallas_call(
        loss_kernel,
        out_shape=(
            jax.ShapeDtypeStruct((classes, seeds), F32),
            jax.ShapeDtypeStruct((1, seeds), F32),
        ),
    )(table.reshape(seeds, hid), labels.reshape(1, seeds))
    return logits, loss.reshape(seeds)


def solution(mesh):
    placed = (
        P("feat", "node"),
        P("feat", "node"),
        P("node"),
        P("node"),
        P("node"),
        P("node", None, None),
        P("node", None),
        P("node"),
        P(None, "feat"),
        P(None, "feat"),
        P(None, "feat"),
        P(None, "feat"),
    )
    return jax.shard_map(
        per_device,
        mesh=mesh,
        in_specs=placed,
        out_specs=(P(None, "node"), P("node")),
        check_vma=False,
    )
```

```python
import functools

import jax
import jax.numpy as jnp
from jax import lax
from jax.experimental import pallas as pl
from jax.experimental.pallas import tpu as pltpu
from jax.sharding import PartitionSpec as P

FAN2 = 10
NX, NZ = 4, 8
LANES = 128
VMEM = 60 * 1024 * 1024
MESH = pl.DeviceIdType.MESH
F32, BF16 = jnp.float32, jnp.bfloat16


def plan_kernel(dst, rows, prev, last, degp):
    slots = 32
    d = dst[...]
    lane = lax.broadcasted_iota(jnp.int32, d.shape, 1)
    pos = lane % slots
    found = jnp.full(d.shape, slots, jnp.int32)
    for s in range(slots - 1, 0, -1):
        found = jnp.where((pos >= s) & (pltpu.roll(d, s, 1) == d), pos - s, found)
    prev[...] = found
    ends = jnp.full(d.shape, slots, jnp.int32)
    for b in range(16):
        v = jnp.where(d == b, pos, -1)
        for s in (1, 2, 4, 8, 16):
            v = jnp.maximum(v, jnp.where((pos & s) == 0, pltpu.roll(v, LANES - s, 1), pltpu.roll(v, s, 1)))
        ends = jnp.where((pos == b) & (v >= 0), v, ends)
    last[...] = ends
    mine = jnp.where(d == lax.axis_index("feat"), rows[...], 0).astype(F32)
    columns = jnp.transpose(jnp.concatenate([mine] * 16, axis=0))
    across = lax.broadcasted_iota(jnp.int32, (LANES, LANES), 1).astype(F32)
    for r in range(8):
        live = jnp.where(across < columns[:, r : r + 1], 1.0, 0.0)
        sums = jnp.sum(live.reshape(4, slots, LANES), axis=1)
        degp[r // 2, (r % 2) * 4 : (r % 2) * 4 + 4, :] = sums


def step_kernel(
    src, rows, prev, last, x_ref, cols, degp, xnear, self1, neigh1, self2, neigh2, nbrs, out,
    xs, cv, buf, parts, stage, weights, wall, a1, b1, a2, b2, ac, ao, bo, bc, dgot, degx, dz_got,
    zs, zr, near, sums, r2, s3, hs, r3, rh, s4, r4,
    csem, wsem, nsem, xsend, xrecv, dsem, esem, zsend, zrecv, fsem, gsend, grecv, psem,
):
    node, f = lax.axis_index("node"), lax.axis_index("feat")
    x, z = node // NZ, node % NZ
    y, core = f // 2, f % 2
    nf = wall.shape[0]
    xp, xm, xo = (x + 1) % NX, (x + NX - 1) % NX, (x + 2) % NX
    half = a1.shape[1]
    body = 2 * half
    slots, depth = cv.shape[2], cv.shape[3]

    def at(xx=x, zz=z, ff=f):
        return {"node": xx * NZ + zz, "feat": ff}

    def send(source, target, send_sem, recv_sem, device):
        copy = pltpu.make_async_remote_copy(
            src_ref=source, dst_ref=target, send_sem=send_sem, recv_sem=recv_sem,
            device_id=device, device_id_type=MESH,
        )
        copy.start()

    def landed(ref, sem):
        pltpu.make_async_copy(ref, ref, sem).wait()

    def order(i):
        return (4 + (1 - 2 * (i % 2)) * ((i + 1) // 2)) % NZ

    def loop(lo, hi, fn):
        lax.fori_loop(lo, hi, lambda i, c: (fn(i), c)[1], 0)

    barrier = pltpu.get_barrier_semaphore()

    def greet(device):
        pl.semaphore_signal(barrier, inc=1, device_id=device, device_id_type=MESH)

    loop(0, NX - 1, lambda i: greet(at(xx=(x + 1 + i) % NX)))
    loop(0, NZ - 1, lambda i: greet(at(zz=(z + 1 + i) % NZ)))
    loop(0, nf - 1, lambda i: greet(at(ff=(f + 1 + i) % nf)))

    def columns_in(i):
        zi = (z + order(i)) % NZ
        pltpu.make_async_copy(cols.at[:, zi], cv.at[:, zi], csem.at[i]).start()

    loop(0, NZ, columns_in)

    for b in range(xs.shape[0]):
        xs[b] = x_ref[:, b * LANES : (b + 1) * LANES].astype(F32)
    buf[...] = jnp.zeros_like(buf)
    for b in range(nf):
        near[b] = xnear[:, b * LANES : (b + 1) * LANES].astype(F32)
    stage[...] = jnp.zeros_like(stage)
    stage[0:8] = self1[...].astype(F32)
    stage[8:16] = neigh1[...].astype(F32)
    stage[16:32, 0 : self2.shape[1]] = self2[...].astype(F32)
    stage[32:48, 0 : neigh2.shape[1]] = neigh2[...].astype(F32)
    weights[...] = stage[...].astype(BF16)
    lane = lax.broadcasted_iota(jnp.int32, (8, LANES), 1)

    def tile_sums(n):
        i, q = n // NX, n % NX
        zi = (z + order(i)) % NZ
        xx = (x + 2 + NX - q) % NX
        base = (xx * NZ + zi) * slots
        for s in range(slots):
            block = xs[src[base + s]]
            got = []
            for k in range(depth):
                index = jnp.broadcast_to(cv[xx, zi, s, pl.ds(k, 1), :], (8, LANES))
                got.append(jnp.take_along_axis(block, index, axis=1, mode="promise_in_bounds"))
            total = functools.reduce(lambda a, b: a + b, got)
            buf[s] = jnp.where(lane < rows[base + s], total, 0.0) + buf[prev[base + s]]
        for b in range(0, nf, 2):
            pair = [buf[last[base + b]], buf[last[base + b + 1]]]
            parts[xx, zi, b * 8 : b * 8 + 16] = jnp.concatenate(pair, axis=0).astype(BF16)

    def first(i):
        zi = (z + order(i)) % NZ
        send(parts.at[xo, zi, pl.ds(0, half)], a1.at[zi], xsend.at[0, zi], xrecv.at[0, zi], at(xx=xp))
        send(parts.at[xo, zi, pl.ds(half, half)], b1.at[zi], xsend.at[1, zi], xrecv.at[1, zi], at(xx=xm))

    def direct_up(i):
        zi = (z + order(i)) % NZ
        send(parts.at[xp, zi, pl.ds(half, half)], bo.at[zi], xsend.at[2, zi], xrecv.at[2, zi], at(xx=xp))

    def direct_down(i):
        zi = (z + order(i)) % NZ
        send(parts.at[xm, zi, pl.ds(0, half)], ao.at[zi], xsend.at[3, zi], xrecv.at[3, zi], at(xx=xm))

    def relay(i):
        zi = (z + order(i)) % NZ
        landed(a1.at[zi], xrecv.at[0, zi])
        a2[zi] = (a1[zi].astype(F32) + parts[xp, zi, pl.ds(0, half), :].astype(F32)).astype(BF16)
        send(a2.at[zi], ac.at[zi], xsend.at[4, zi], xrecv.at[4, zi], at(xx=xp))
        landed(b1.at[zi], xrecv.at[1, zi])
        b2[zi] = (b1[zi].astype(F32) + parts[xm, zi, pl.ds(half, half), :].astype(F32)).astype(BF16)
        send(b2.at[zi], bc.at[zi], xsend.at[5, zi], xrecv.at[5, zi], at(xx=xm))

    def summed(i):
        zi = (z + order(i)) % NZ
        for kind, ref in ((2, bo), (3, ao), (4, ac), (5, bc)):
            landed(ref.at[zi], xrecv.at[kind, zi])
        upper = parts[x, zi, pl.ds(0, half), :].astype(F32) + ao[zi].astype(F32) + ac[zi].astype(F32)
        lower = parts[x, zi, pl.ds(half, half), :].astype(F32) + bo[zi].astype(F32) + bc[zi].astype(F32)
        return upper, lower

    def onward(i):
        dz = order(i)
        zi = (z + dz) % NZ
        upper, lower = summed(i)
        zs[dz - 1, 0:half] = upper.astype(BF16)
        zs[dz - 1, half:body] = lower.astype(BF16)
        send(zs.at[dz - 1], zr.at[dz - 1], zsend.at[dz - 1], zrecv.at[dz - 1], at(zz=zi))

    loop(0, NX, lambda n: (pl.when(n == 0)(lambda: landed(cv.at[:, 0], csem.at[0])), tile_sums(n)))

    pl.semaphore_wait(barrier, NX - 1 + NZ - 1 + nf - 1)
    first(0)
    for i in range(NX - 1):
        send(degp.at[(x + 1 + i) % NX], dgot.at[i], dsem.at[0, i], dsem.at[1, i], at(xx=(x + 1 + i) % NX))
    direct_up(0)
    direct_down(0)

    wall[f] = weights[...]
    r2[f, 0:8] = near[f]

    def early(i):
        p = (f + 1 + i) % nf
        send(near.at[p], r2.at[f, pl.ds(0, 8)], nsem.at[0, 0], nsem.at[1, f], at(ff=p))
        send(weights, wall.at[f], wsem.at[0], wsem.at[1], at(ff=p))

    loop(0, nf - 1, early)

    def step(n):
        i, q = n // NX, n % NX

        @pl.when(q == 0)
        def _():
            landed(cv.at[:, 0], csem.at[i])

        tile_sums(n)

        @pl.when(q == 0)
        def _():
            first(i)

        @pl.when(q == 1)
        def _():
            direct_up(i)
            relay(i - 1)

        @pl.when((q == 2) & (i >= 2))
        def _():
            onward(i - 2)

        @pl.when(q == 3)
        def _():
            direct_down(i)

        @pl.when(n == NX + 3)
        def _():
            for j in range(NX - 1):
                landed(dgot.at[j], dsem.at[1, j])
            degx[...] = degp[x] + dgot[0] + dgot[1] + dgot[2]
            for dz in range(1, NZ):
                send(degx, dz_got.at[dz - 1], esem.at[0, dz - 1], esem.at[1, dz - 1], at(zz=(z + dz) % NZ))

    loop(NX, NX * NZ, step)
    relay(NZ - 1)
    onward(NZ - 2)

    own_nodes = lax.broadcasted_iota(jnp.int32, (LANES, nbrs.shape[1]), 0) + f * LANES
    counts = jnp.zeros(own_nodes.shape, F32)
    for n in range(FAN2):
        counts += jnp.where(nbrs[n : n + 1, :] == own_nodes, 1.0, 0.0)
    counts = counts.astype(BF16)
    deg = degx[pl.ds(z, 1), :]
    for i in range(NZ - 1):
        landed(dz_got.at[i], esem.at[1, i])
        deg += dz_got[i, pl.ds(z, 1), :]
    deg = jnp.maximum(4.0 * deg, 1.0)

    upper, lower = summed(NZ - 1)
    for i in (3, 2, 4, 1, 5, 0, 6):
        landed(zr.at[i], zrecv.at[i])
        upper += zr[i, 0:half].astype(F32)
        lower += zr[i, half:body].astype(F32)
    for b in range(nf // 2):
        sums[b] = upper[b * 8 : b * 8 + 8]
        sums[b + nf // 2] = lower[b * 8 : b * 8 + 8]

    def spread(i):
        p = (f + 1 + i) % nf
        send(sums.at[p], r2.at[f, pl.ds(8, 8)], fsem.at[0], fsem.at[1], at(ff=p))

    loop(0, nf - 1, spread)
    r2[f, 8:16] = sums[f]
    landed(wall.at[pl.ds(0, nf - 1)], wsem.at[1])

    def near_in(i):
        p = (f + 1 + i) % nf
        landed(near.at[p], nsem.at[1, p])

    loop(0, nf - 1, near_in)
    landed(sums.at[pl.ds(0, nf - 1)], fsem.at[1])
    both = r2[...].reshape(nf * 16, LANES)
    is_sum = lax.broadcasted_iota(jnp.int32, both.shape, 0) % 16 >= 8
    both = jnp.where(is_sum, both / deg, both).astype(BF16)
    w1 = wall[:, 0:16, :].reshape(nf * 16, wall.shape[2])
    pre = lax.dot_general(both, w1, (((0,), (0,)), ((), ())), preferred_element_type=F32)
    hidden = jnp.maximum(pre, 0.0).astype(BF16)
    seed_sums = lax.dot_general(counts, hidden, (((0,), (0,)), ((), ())), preferred_element_type=F32)
    for p in range(nf):
        piece = seed_sums[p * 8 : p * 8 + 8]
        s3[p] = jnp.concatenate([piece[:, 0:LANES], piece[:, LANES:]], axis=0).astype(BF16)

    @pl.when(f == 0)
    def _():
        wide = hidden.astype(F32)
        for p in range(nf):
            piece = wide[p * 8 : p * 8 + 8]
            hs[p] = jnp.concatenate([piece[:, 0:LANES], piece[:, LANES:]], axis=0).astype(BF16)

    def seeds_out(i):
        p = (f + 1 + i) % nf
        send(s3.at[p], r3.at[f], fsem.at[2], fsem.at[3], at(ff=p))

        @pl.when(f == 0)
        def _():
            send(hs.at[p], rh, fsem.at[4], fsem.at[5], at(ff=p))

    loop(0, nf - 1, seeds_out)
    r3[f] = s3[f]

    @pl.when(f == 0)
    def _():
        rh[...] = hs[0]

    @pl.when(f != 0)
    def _():
        landed(rh, fsem.at[5])

    w2s = wall[:, 16:32, :].reshape(nf * 16, wall.shape[2])
    w2n = wall[:, 32:48, :].reshape(nf * 16, wall.shape[2])

    def rejoin(v):
        return jnp.concatenate([v[0:8], v[8:16]], axis=1).astype(BF16)

    logits = jnp.dot(rejoin(rh[...].astype(F32)), w2s, preferred_element_type=F32)
    landed(s3.at[pl.ds(0, nf - 1)], fsem.at[3])
    mean = jnp.zeros(r3.shape[1:], F32)
    for p in range(nf):
        mean += r3[p].astype(F32)
    logits += jnp.dot(rejoin(mean / FAN2), w2n, preferred_element_type=F32)

    s4[...] = logits
    other = at(ff=f + 1 - 2 * core)

    def along(i):
        yy = (y + 1 + i) % (nf // 2)
        send(s4, r4.at[core, y], gsend.at[i], grecv.at[y], at(ff=yy * 2 + core))

    loop(0, nf // 2 - 1, along)
    send(s4, r4.at[core, y], gsend.at[nf // 2 - 1], psem.at[1, y], other)
    r4[core, y] = logits

    def across(i):
        yy = (y + nf + (1 - 2 * (i % 2)) * (i // 2 + 1)) % (nf // 2)
        landed(s4, grecv.at[yy])
        send(r4.at[core, yy], r4.at[core, yy], psem.at[0, i], psem.at[1, yy], other)

    loop(0, nf // 2 - 1, across)

    def sent(i):
        for kind, ref in ((0, a1), (1, b1), (2, bo), (3, ao), (4, ac), (5, bc)):
            landed(ref.at[i], xsend.at[kind, i])

    loop(0, NZ, sent)
    for i in range(NX - 1):
        landed(dgot.at[i], dsem.at[0, i])
    for i in range(NZ - 1):
        landed(zr.at[i], zsend.at[i])
        landed(dz_got.at[i], esem.at[0, i])
    landed(wall.at[pl.ds(0, nf - 1)], wsem.at[0])
    landed(near.at[pl.ds(0, nf - 1)], nsem.at[0, 0])
    landed(sums.at[pl.ds(0, nf - 1)], fsem.at[0])
    landed(s3.at[pl.ds(0, nf - 1)], fsem.at[2])

    @pl.when(f == 0)
    def _():
        landed(hs.at[pl.ds(0, nf - 1)], fsem.at[4])

    for i in range(nf // 2):
        landed(s4, gsend.at[i])
        landed(s4, psem.at[1, i])
    for i in range(nf // 2 - 1):
        landed(s4, psem.at[0, i])
    for i in range(nf):
        out[i] = r4[i % 2, i // 2]


def tile_plan(dst, rows):
    shape = (8, LANES)
    ints = jax.ShapeDtypeStruct(shape, jnp.int32)
    return pl.pallas_call(
        plan_kernel,
        out_shape=(ints, ints, jax.ShapeDtypeStruct((NX, NZ, LANES), F32)),
        compiler_params=pltpu.CompilerParams(vmem_limit_bytes=VMEM),
    )(dst.reshape(shape), rows.reshape(shape))


def seed_logits(src, rows, x, cols, degp, prev, last, xnear, w, nbrs, feats):
    self1, neigh1, self2, neigh2 = w
    hid = self1.shape[1]
    seeds = nbrs.shape[1]
    slots, depth = cols.shape[0] // (NX * NZ), cols.shape[1]
    body = feats * 8
    half = body // 2
    vm = pl.BlockSpec(memory_space=pltpu.VMEM)
    sm = pl.BlockSpec(memory_space=pltpu.SMEM)
    quarter = pltpu.VMEM((NZ, half, LANES), BF16)
    dma = pltpu.SemaphoreType.DMA
    return pl.pallas_call(
        step_kernel,
        out_shape=jax.ShapeDtypeStruct((feats, seeds // feats, hid), F32),
        in_specs=[sm] * 4 + [vm, pl.BlockSpec(memory_space=pl.ANY)] + [vm] * 7,
        out_specs=vm,
        scratch_shapes=[
            pltpu.VMEM((x.shape[1] // LANES, 8, LANES), F32),
            pltpu.VMEM((NX, NZ, slots, depth, LANES), jnp.int32),
            pltpu.VMEM((slots + 1, 8, LANES), F32),
            pltpu.VMEM((NX, NZ, body, LANES), BF16),
            pltpu.VMEM((48, hid), F32),
            pltpu.VMEM((48, hid), BF16),
            pltpu.VMEM((feats, 48, hid), BF16),
            *[quarter] * 8,
            pltpu.VMEM((NX - 1, NZ, LANES), F32),
            pltpu.VMEM((NZ, LANES), F32),
            pltpu.VMEM((NZ - 1, NZ, LANES), F32),
            pltpu.VMEM((NZ - 1, body, LANES), BF16),
            pltpu.VMEM((NZ - 1, body, LANES), BF16),
            pltpu.VMEM((feats, 8, LANES), F32),
            pltpu.VMEM((feats, 8, LANES), F32),
            pltpu.VMEM((feats, 16, LANES), F32),
            pltpu.VMEM((feats, 16, LANES), BF16),
            pltpu.VMEM((feats, 16, LANES), BF16),
            pltpu.VMEM((feats, 16, LANES), BF16),
            pltpu.VMEM((16, LANES), BF16),
            pltpu.VMEM((8, hid), F32),
            pltpu.VMEM((2, feats // 2, 8, hid), F32),
            dma((NZ,)),
            dma((2,)),
            dma((2, feats)),
            dma((6, NZ)),
            dma((6, NZ)),
            dma((2, NX - 1)),
            dma((2, NZ - 1)),
            dma((NZ - 1,)),
            dma((NZ - 1,)),
            dma((6,)),
            dma((feats // 2,)),
            dma((feats // 2,)),
            dma((2, feats // 2)),
        ],
        compiler_params=pltpu.CompilerParams(
            collective_id=0, has_side_effects=True, vmem_limit_bytes=VMEM
        ),
    )(
        src, rows, prev.reshape(-1), last.reshape(-1), x, cols.reshape(NX, NZ, slots, depth, LANES),
        degp, xnear, self1, neigh1, self2, neigh2, nbrs,
    )


def loss_kernel(table, labels, logits, loss):
    full = jnp.transpose(table[...])
    rows = full[0 : logits.shape[0]]
    logits[...] = rows
    classes = lax.broadcasted_iota(jnp.int32, rows.shape, 0)
    picked = jnp.sum(jnp.where(classes == labels[...], rows, 0.0), axis=0, keepdims=True)
    loss[...] = jnp.log(jnp.sum(jnp.exp(rows), axis=0, keepdims=True)) - picked


def per_device(
    x_far,
    x_near,
    tile_src,
    tile_dst,
    tile_rows,
    tile_cols,
    seed_nbrs,
    labels,
    self_one,
    neigh_one,
    self_two,
    neigh_two,
):
    feats = lax.axis_size("feat")
    classes, hid = self_two.shape[0], self_one.shape[0]
    seeds = labels.shape[0]
    prev, last, degp = tile_plan(tile_dst, tile_rows)
    weights = (self_one.T, neigh_one.T, self_two.T, neigh_two.T)
    table = seed_logits(
        tile_src, tile_rows, x_far, tile_cols, degp, prev, last, x_near, weights, seed_nbrs.T, feats
    )
    logits, loss = pl.pallas_call(
        loss_kernel,
        out_shape=(
            jax.ShapeDtypeStruct((classes, seeds), F32),
            jax.ShapeDtypeStruct((1, seeds), F32),
        ),
        compiler_params=pltpu.CompilerParams(vmem_limit_bytes=VMEM),
    )(table.reshape(seeds, hid), labels.reshape(1, seeds))
    return logits, loss.reshape(seeds)


def solution(mesh):
    placed = (
        P("feat", "node"),
        P("feat", "node"),
        P("node"),
        P("node"),
        P("node"),
        P("node", None, None),
        P("node", None),
        P("node"),
        P(None, "feat"),
        P(None, "feat"),
        P(None, "feat"),
        P(None, "feat"),
    )
    return jax.shard_map(
        per_device,
        mesh=mesh,
        in_specs=placed,
        out_specs=(P(None, "node"), P("node")),
        check_vma=False,
    )
```

```python
import functools

import jax
import jax.numpy as jnp
from jax import lax
from jax.experimental import pallas as pl
from jax.experimental.pallas import tpu as pltpu
from jax.sharding import PartitionSpec as P

FAN2 = 10
NX, NZ = 4, 8
LANES = 128
VMEM = 60 * 1024 * 1024
MESH = pl.DeviceIdType.MESH
F32, BF16 = jnp.float32, jnp.bfloat16


def plan_kernel(dst, rows, prev, last, degp):
    slots = 32
    d = dst[...]
    lane = lax.broadcasted_iota(jnp.int32, d.shape, 1)
    pos = lane % slots
    found = jnp.full(d.shape, slots, jnp.int32)
    for s in range(slots - 1, 0, -1):
        found = jnp.where((pos >= s) & (pltpu.roll(d, s, 1) == d), pos - s, found)
    prev[...] = found
    ends = jnp.full(d.shape, slots, jnp.int32)
    for b in range(16):
        v = jnp.where(d == b, pos, -1)
        for s in (1, 2, 4, 8, 16):
            v = jnp.maximum(v, jnp.where((pos & s) == 0, pltpu.roll(v, LANES - s, 1), pltpu.roll(v, s, 1)))
        ends = jnp.where((pos == b) & (v >= 0), v, ends)
    last[...] = ends
    mine = jnp.where(d == lax.axis_index("feat"), rows[...], 0).astype(F32)
    columns = jnp.transpose(jnp.concatenate([mine] * 16, axis=0))
    across = lax.broadcasted_iota(jnp.int32, (LANES, LANES), 1).astype(F32)
    for r in range(8):
        live = jnp.where(across < columns[:, r : r + 1], 1.0, 0.0)
        sums = jnp.sum(live.reshape(4, slots, LANES), axis=1)
        degp[r // 2, (r % 2) * 4 : (r % 2) * 4 + 4, :] = sums


def step_kernel(
    src, rows, prev, last, x_ref, cols, degp, xnear, self1, neigh1, self2, neigh2, nbrs, out,
    xs, cv, buf, parts, stage, weights, wall, a1, b1, a2, b2, ac, ao, bo, bc, dgot, degx, dz_got,
    zs, zr, near, sums, r2, s3, hs, r3, rh, s4, r4,
    csem, wsem, nsem, xsend, xrecv, dsem, esem, zsend, zrecv, fsem, gsend, grecv, psem,
):
    node, f = lax.axis_index("node"), lax.axis_index("feat")
    x, z = node // NZ, node % NZ
    y, core = f // 2, f % 2
    nf = wall.shape[0]
    xp, xm, xo = (x + 1) % NX, (x + NX - 1) % NX, (x + 2) % NX
    half = a1.shape[1]
    body = 2 * half
    slots, depth = cv.shape[2], cv.shape[3]

    def at(xx=x, zz=z, ff=f):
        return {"node": xx * NZ + zz, "feat": ff}

    def send(source, target, send_sem, recv_sem, device):
        copy = pltpu.make_async_remote_copy(
            src_ref=source, dst_ref=target, send_sem=send_sem, recv_sem=recv_sem,
            device_id=device, device_id_type=MESH,
        )
        copy.start()

    def landed(ref, sem):
        pltpu.make_async_copy(ref, ref, sem).wait()

    def order(i):
        return (4 + (1 - 2 * (i % 2)) * ((i + 1) // 2)) % NZ

    def loop(lo, hi, fn):
        lax.fori_loop(lo, hi, lambda i, c: (fn(i), c)[1], 0)

    barrier = pltpu.get_barrier_semaphore()

    def greet(device):
        pl.semaphore_signal(barrier, inc=1, device_id=device, device_id_type=MESH)

    loop(0, NX - 1, lambda i: greet(at(xx=(x + 1 + i) % NX)))
    loop(0, NZ - 1, lambda i: greet(at(zz=(z + 1 + i) % NZ)))
    loop(0, nf - 1, lambda i: greet(at(ff=(f + 1 + i) % nf)))

    def columns_in(i):
        zi = (z + order(i)) % NZ
        pltpu.make_async_copy(cols.at[:, zi], cv.at[:, zi], csem.at[i]).start()

    loop(0, NZ, columns_in)

    for b in range(xs.shape[0]):
        xs[b] = x_ref[:, b * LANES : (b + 1) * LANES].astype(F32)
    buf[...] = jnp.zeros_like(buf)
    for b in range(nf):
        near[b] = xnear[:, b * LANES : (b + 1) * LANES].astype(F32)
    stage[...] = jnp.zeros_like(stage)
    stage[0:8] = self1[...].astype(F32)
    stage[8:16] = neigh1[...].astype(F32)
    stage[16:32, 0 : self2.shape[1]] = self2[...].astype(F32)
    stage[32:48, 0 : neigh2.shape[1]] = neigh2[...].astype(F32)
    weights[...] = stage[...].astype(BF16)
    lane = lax.broadcasted_iota(jnp.int32, (8, LANES), 1)

    rows_of = lax.broadcasted_iota(jnp.int32, (16, LANES), 0)
    ids = [(rows_of + 16 * g).astype(jnp.int16) for g in range(LANES // 16)]
    one, zero = jnp.ones((16, LANES), BF16), jnp.zeros((16, LANES), BF16)

    def gathered(block, xx, zi, s):
        got = []
        for k in range(depth):
            index = jnp.broadcast_to(cv[xx, zi, s, pl.ds(k, 1), :], (8, LANES))
            got.append(jnp.take_along_axis(block, index, axis=1, mode="promise_in_bounds"))
        return functools.reduce(lambda a, b: a + b, got)

    def counted(block, xx, zi, s):
        index = [
            jnp.broadcast_to(cv[xx, zi, s, pl.ds(k, 1), :], (16, LANES)).astype(jnp.int16)
            for k in range(depth)
        ]
        groups = []
        for g in ids:
            hits = [jnp.where(row == g, one, zero) for row in index]
            groups.append(functools.reduce(lambda a, b: a + b, hits))
        matrix = jnp.concatenate(groups, axis=0)
        return jnp.dot(block.astype(BF16), matrix, preferred_element_type=F32)

    def tile_sums(xx, zi):
        base = (xx * NZ + zi) * slots
        for s in range(slots):
            block = xs[src[base + s]]
            total = (counted if s % 2 else gathered)(block, xx, zi, s)
            buf[s] = jnp.where(lane < rows[base + s], total, 0.0) + buf[prev[base + s]]
        for b in range(0, nf, 2):
            pair = [buf[last[base + b]], buf[last[base + b + 1]]]
            parts[xx, zi, b * 8 : b * 8 + 16] = jnp.concatenate(pair, axis=0).astype(BF16)

    def first(i):
        zi = (z + order(i)) % NZ
        send(parts.at[xo, zi, pl.ds(0, half)], a1.at[zi], xsend.at[0, zi], xrecv.at[0, zi], at(xx=xp))
        send(parts.at[xo, zi, pl.ds(half, half)], b1.at[zi], xsend.at[1, zi], xrecv.at[1, zi], at(xx=xm))

    def direct_up(i):
        zi = (z + order(i)) % NZ
        send(parts.at[xp, zi, pl.ds(half, half)], bo.at[zi], xsend.at[2, zi], xrecv.at[2, zi], at(xx=xp))

    def direct_down(i):
        zi = (z + order(i)) % NZ
        send(parts.at[xm, zi, pl.ds(0, half)], ao.at[zi], xsend.at[3, zi], xrecv.at[3, zi], at(xx=xm))

    def relay_up(i):
        zi = (z + order(i)) % NZ
        landed(a1.at[zi], xrecv.at[0, zi])
        a2[zi] = (a1[zi].astype(F32) + parts[xp, zi, pl.ds(0, half), :].astype(F32)).astype(BF16)
        send(a2.at[zi], ac.at[zi], xsend.at[4, zi], xrecv.at[4, zi], at(xx=xp))

    def relay_down(i):
        zi = (z + order(i)) % NZ
        landed(b1.at[zi], xrecv.at[1, zi])
        b2[zi] = (b1[zi].astype(F32) + parts[xm, zi, pl.ds(half, half), :].astype(F32)).astype(BF16)
        send(b2.at[zi], bc.at[zi], xsend.at[5, zi], xrecv.at[5, zi], at(xx=xm))

    def summed(i):
        zi = (z + order(i)) % NZ
        for kind, ref in ((2, bo), (3, ao), (4, ac), (5, bc)):
            landed(ref.at[zi], xrecv.at[kind, zi])
        upper = parts[x, zi, pl.ds(0, half), :].astype(F32) + ao[zi].astype(F32) + ac[zi].astype(F32)
        lower = parts[x, zi, pl.ds(half, half), :].astype(F32) + bo[zi].astype(F32) + bc[zi].astype(F32)
        return upper, lower

    def onward(i):
        dz = order(i)
        zi = (z + dz) % NZ
        upper, lower = summed(i)
        zs[dz - 1, 0:half] = upper.astype(BF16)
        zs[dz - 1, half:body] = lower.astype(BF16)
        send(zs.at[dz - 1], zr.at[dz - 1], zsend.at[dz - 1], zrecv.at[dz - 1], at(zz=zi))

    def far(i):
        landed(cv.at[:, 0], csem.at[i])
        tile_sums(xo, (z + order(i)) % NZ)

    loop(0, NZ, far)
    pl.semaphore_wait(barrier, NX - 1 + NZ - 1 + nf - 1)
    loop(0, NZ, first)
    for i in range(NX - 1):
        send(degp.at[(x + 1 + i) % NX], dgot.at[i], dsem.at[0, i], dsem.at[1, i], at(xx=(x + 1 + i) % NX))

    wall[f] = weights[...]
    r2[f, 0:8] = near[f]

    def early(i):
        p = (f + 1 + i) % nf
        send(near.at[p], r2.at[f, pl.ds(0, 8)], nsem.at[0, 0], nsem.at[1, f], at(ff=p))
        send(weights, wall.at[f], wsem.at[0], wsem.at[1], at(ff=p))

    loop(0, nf - 1, early)

    lag = 3

    def step(n):
        i, q = n // 3, n % 3
        tile_sums((x + 1 + 2 * q + 3 * (q // 2)) % NX, (z + order(i)) % NZ)

        @pl.when(q == 0)
        def _():
            direct_up(i)
            relay_up(i)

        @pl.when(q == 1)
        def _():
            direct_down(i)
            relay_down(i)

        @pl.when((q == 2) & (i >= lag))
        def _():
            onward(i - lag)

        @pl.when(n == 7)
        def _():
            for j in range(NX - 1):
                landed(dgot.at[j], dsem.at[1, j])
            degx[...] = degp[x] + dgot[0] + dgot[1] + dgot[2]
            for dz in range(1, NZ):
                send(degx, dz_got.at[dz - 1], esem.at[0, dz - 1], esem.at[1, dz - 1], at(zz=(z + dz) % NZ))

    loop(0, 3 * NZ, step)
    loop(NZ - lag, NZ - 1, onward)

    own_nodes = lax.broadcasted_iota(jnp.int32, (LANES, nbrs.shape[1]), 0) + f * LANES
    counts = jnp.zeros(own_nodes.shape, F32)
    for n in range(FAN2):
        counts += jnp.where(nbrs[n : n + 1, :] == own_nodes, 1.0, 0.0)
    counts = jnp.transpose(counts).astype(BF16)
    deg = degx[pl.ds(z, 1), :]
    for i in range(NZ - 1):
        landed(dz_got.at[i], esem.at[1, i])
        deg += dz_got[i, pl.ds(z, 1), :]
    deg = jnp.maximum(4.0 * deg, 1.0)

    upper, lower = summed(NZ - 1)
    for i in (3, 2, 4, 1, 5, 0, 6):
        landed(zr.at[i], zrecv.at[i])
        upper += zr[i, 0:half].astype(F32)
        lower += zr[i, half:body].astype(F32)
    for b in range(nf // 2):
        sums[b] = upper[b * 8 : b * 8 + 8]
        sums[b + nf // 2] = lower[b * 8 : b * 8 + 8]

    def spread(i):
        p = (f + 1 + i) % nf
        send(sums.at[p], r2.at[f, pl.ds(8, 8)], fsem.at[0], fsem.at[1], at(ff=p))

    loop(0, nf - 1, spread)
    r2[f, 8:16] = sums[f]
    landed(wall.at[pl.ds(0, nf - 1)], wsem.at[1])

    def near_in(i):
        p = (f + 1 + i) % nf
        landed(near.at[p], nsem.at[1, p])

    loop(0, nf - 1, near_in)
    landed(sums.at[pl.ds(0, nf - 1)], fsem.at[1])
    both = r2[...].reshape(nf * 16, LANES)
    is_sum = lax.broadcasted_iota(jnp.int32, both.shape, 0) % 16 >= 8
    both = jnp.where(is_sum, both / deg, both).astype(BF16)
    w1 = wall[:, 0:16, :].reshape(nf * 16, wall.shape[2])
    pre = lax.dot_general(both, w1, (((0,), (0,)), ((), ())), preferred_element_type=F32)
    hidden = jnp.maximum(pre, 0.0).astype(BF16)
    seed_sums = jnp.dot(counts, hidden, preferred_element_type=F32)
    for p in range(nf):
        piece = seed_sums[p * 8 : p * 8 + 8]
        s3[p] = jnp.concatenate([piece[:, 0:LANES], piece[:, LANES:]], axis=0).astype(BF16)

    @pl.when(f == 0)
    def _():
        wide = hidden.astype(F32)
        for p in range(nf):
            piece = wide[p * 8 : p * 8 + 8]
            hs[p] = jnp.concatenate([piece[:, 0:LANES], piece[:, LANES:]], axis=0).astype(BF16)

    def seeds_out(i):
        p = (f + 1 + i) % nf
        send(s3.at[p], r3.at[f], fsem.at[2], fsem.at[3], at(ff=p))

        @pl.when(f == 0)
        def _():
            send(hs.at[p], rh, fsem.at[4], fsem.at[5], at(ff=p))

    loop(0, nf - 1, seeds_out)
    r3[f] = s3[f]

    @pl.when(f == 0)
    def _():
        rh[...] = hs[0]

    @pl.when(f != 0)
    def _():
        landed(rh, fsem.at[5])

    w2s = wall[:, 16:32, :].reshape(nf * 16, wall.shape[2])
    w2n = wall[:, 32:48, :].reshape(nf * 16, wall.shape[2])

    def rejoin(v):
        return jnp.concatenate([v[0:8], v[8:16]], axis=1).astype(BF16)

    logits = jnp.dot(rejoin(rh[...].astype(F32)), w2s, preferred_element_type=F32)
    landed(s3.at[pl.ds(0, nf - 1)], fsem.at[3])
    mean = jnp.zeros(r3.shape[1:], F32)
    for p in range(nf):
        mean += r3[p].astype(F32)
    logits += jnp.dot(rejoin(mean / FAN2), w2n, preferred_element_type=F32)

    s4[...] = logits
    other = at(ff=f + 1 - 2 * core)

    def along(i):
        yy = (y + 1 + i) % (nf // 2)
        send(s4, r4.at[core, y], gsend.at[i], grecv.at[y], at(ff=yy * 2 + core))

    loop(0, nf // 2 - 1, along)
    send(s4, r4.at[core, y], gsend.at[nf // 2 - 1], psem.at[1, y], other)
    r4[core, y] = logits

    def across(i):
        yy = (y + nf + (1 - 2 * (i % 2)) * (i // 2 + 1)) % (nf // 2)
        landed(s4, grecv.at[yy])
        send(r4.at[core, yy], r4.at[core, yy], psem.at[0, i], psem.at[1, yy], other)

    loop(0, nf // 2 - 1, across)

    def sent(i):
        for kind, ref in ((0, a1), (1, b1), (2, bo), (3, ao), (4, ac), (5, bc)):
            landed(ref.at[i], xsend.at[kind, i])

    loop(0, NZ, sent)
    for i in range(NX - 1):
        landed(dgot.at[i], dsem.at[0, i])
    for i in range(NZ - 1):
        landed(zr.at[i], zsend.at[i])
        landed(dz_got.at[i], esem.at[0, i])
    landed(wall.at[pl.ds(0, nf - 1)], wsem.at[0])
    landed(near.at[pl.ds(0, nf - 1)], nsem.at[0, 0])
    landed(sums.at[pl.ds(0, nf - 1)], fsem.at[0])
    landed(s3.at[pl.ds(0, nf - 1)], fsem.at[2])

    @pl.when(f == 0)
    def _():
        landed(hs.at[pl.ds(0, nf - 1)], fsem.at[4])

    for i in range(nf // 2):
        landed(s4, gsend.at[i])
        landed(s4, psem.at[1, i])
    for i in range(nf // 2 - 1):
        landed(s4, psem.at[0, i])
    for i in range(nf):
        out[i] = r4[i % 2, i // 2]


def tile_plan(dst, rows):
    shape = (8, LANES)
    ints = jax.ShapeDtypeStruct(shape, jnp.int32)
    return pl.pallas_call(
        plan_kernel,
        out_shape=(ints, ints, jax.ShapeDtypeStruct((NX, NZ, LANES), F32)),
        compiler_params=pltpu.CompilerParams(vmem_limit_bytes=VMEM),
    )(dst.reshape(shape), rows.reshape(shape))


def seed_logits(src, rows, x, cols, degp, prev, last, xnear, w, nbrs, feats):
    self1, neigh1, self2, neigh2 = w
    hid = self1.shape[1]
    seeds = nbrs.shape[1]
    slots, depth = cols.shape[0] // (NX * NZ), cols.shape[1]
    body = feats * 8
    half = body // 2
    vm = pl.BlockSpec(memory_space=pltpu.VMEM)
    sm = pl.BlockSpec(memory_space=pltpu.SMEM)
    quarter = pltpu.VMEM((NZ, half, LANES), BF16)
    dma = pltpu.SemaphoreType.DMA
    return pl.pallas_call(
        step_kernel,
        out_shape=jax.ShapeDtypeStruct((feats, seeds // feats, hid), F32),
        in_specs=[sm] * 4 + [vm, pl.BlockSpec(memory_space=pl.ANY)] + [vm] * 7,
        out_specs=vm,
        scratch_shapes=[
            pltpu.VMEM((x.shape[1] // LANES, 8, LANES), F32),
            pltpu.VMEM((NX, NZ, slots, depth, LANES), jnp.int32),
            pltpu.VMEM((slots + 1, 8, LANES), F32),
            pltpu.VMEM((NX, NZ, body, LANES), BF16),
            pltpu.VMEM((48, hid), F32),
            pltpu.VMEM((48, hid), BF16),
            pltpu.VMEM((feats, 48, hid), BF16),
            *[quarter] * 8,
            pltpu.VMEM((NX - 1, NZ, LANES), F32),
            pltpu.VMEM((NZ, LANES), F32),
            pltpu.VMEM((NZ - 1, NZ, LANES), F32),
            pltpu.VMEM((NZ - 1, body, LANES), BF16),
            pltpu.VMEM((NZ - 1, body, LANES), BF16),
            pltpu.VMEM((feats, 8, LANES), F32),
            pltpu.VMEM((feats, 8, LANES), F32),
            pltpu.VMEM((feats, 16, LANES), F32),
            pltpu.VMEM((feats, 16, LANES), BF16),
            pltpu.VMEM((feats, 16, LANES), BF16),
            pltpu.VMEM((feats, 16, LANES), BF16),
            pltpu.VMEM((16, LANES), BF16),
            pltpu.VMEM((8, hid), F32),
            pltpu.VMEM((2, feats // 2, 8, hid), F32),
            dma((NZ,)),
            dma((2,)),
            dma((2, feats)),
            dma((6, NZ)),
            dma((6, NZ)),
            dma((2, NX - 1)),
            dma((2, NZ - 1)),
            dma((NZ - 1,)),
            dma((NZ - 1,)),
            dma((6,)),
            dma((feats // 2,)),
            dma((feats // 2,)),
            dma((2, feats // 2)),
        ],
        compiler_params=pltpu.CompilerParams(
            collective_id=0, has_side_effects=True, vmem_limit_bytes=VMEM
        ),
    )(
        src, rows, prev.reshape(-1), last.reshape(-1), x, cols.reshape(NX, NZ, slots, depth, LANES),
        degp, xnear, self1, neigh1, self2, neigh2, nbrs,
    )


def loss_kernel(table, labels, logits, loss):
    full = jnp.transpose(table[...])
    rows = full[0 : logits.shape[0]]
    logits[...] = rows
    classes = lax.broadcasted_iota(jnp.int32, rows.shape, 0)
    picked = jnp.sum(jnp.where(classes == labels[...], rows, 0.0), axis=0, keepdims=True)
    loss[...] = jnp.log(jnp.sum(jnp.exp(rows), axis=0, keepdims=True)) - picked


def per_device(
    x_far,
    x_near,
    tile_src,
    tile_dst,
    tile_rows,
    tile_cols,
    seed_nbrs,
    labels,
    self_one,
    neigh_one,
    self_two,
    neigh_two,
):
    feats = lax.axis_size("feat")
    classes, hid = self_two.shape[0], self_one.shape[0]
    seeds = labels.shape[0]
    prev, last, degp = tile_plan(tile_dst, tile_rows)
    weights = (self_one.T, neigh_one.T, self_two.T, neigh_two.T)
    table = seed_logits(
        tile_src, tile_rows, x_far, tile_cols, degp, prev, last, x_near, weights, seed_nbrs.T, feats
    )
    logits, loss = pl.pallas_call(
        loss_kernel,
        out_shape=(
            jax.ShapeDtypeStruct((classes, seeds), F32),
            jax.ShapeDtypeStruct((1, seeds), F32),
        ),
        compiler_params=pltpu.CompilerParams(vmem_limit_bytes=VMEM),
    )(table.reshape(seeds, hid), labels.reshape(1, seeds))
    return logits, loss.reshape(seeds)


def solution(mesh):
    placed = (
        P("feat", "node"),
        P("feat", "node"),
        P("node"),
        P("node"),
        P("node"),
        P("node", None, None),
        P("node", None),
        P("node"),
        P(None, "feat"),
        P(None, "feat"),
        P(None, "feat"),
        P(None, "feat"),
    )
    return jax.shard_map(
        per_device,
        mesh=mesh,
        in_specs=placed,
        out_specs=(P(None, "node"), P("node")),
        check_vma=False,
    )
```

```python
import functools

import jax
import jax.numpy as jnp
from jax import lax
from jax.experimental import pallas as pl
from jax.experimental.pallas import tpu as pltpu
from jax.sharding import PartitionSpec as P

FAN2 = 10
NX, NZ = 4, 8
LANES = 128
VMEM = 60 * 1024 * 1024
MESH = pl.DeviceIdType.MESH
F32, BF16 = jnp.float32, jnp.bfloat16


def slot_plan(d):
    slots = 32
    pos = lax.broadcasted_iota(jnp.int32, d.shape, 1) % slots
    prev = jnp.full(d.shape, slots, jnp.int32)
    for s in range(slots - 1, 0, -1):
        prev = jnp.where((pos >= s) & (pltpu.roll(d, s, 1) == d), pos - s, prev)
    last = jnp.full(d.shape, slots, jnp.int32)
    for b in range(16):
        v = jnp.where(d == b, pos, -1)
        for s in (1, 2, 4, 8, 16):
            v = jnp.maximum(v, jnp.where((pos & s) == 0, pltpu.roll(v, LANES - s, 1), pltpu.roll(v, s, 1)))
        last = jnp.where((pos == b) & (v >= 0), v, last)
    return prev, last


def block_counts(rows, degp):
    columns = jnp.transpose(jnp.concatenate([rows.astype(F32)] * 16, axis=0))
    across = lax.broadcasted_iota(jnp.int32, (LANES, LANES), 1).astype(F32)
    for r in range(8):
        live = jnp.where(across < columns[:, r : r + 1], 1.0, 0.0)
        sums = jnp.sum(live.reshape(4, LANES // 4, LANES), axis=1)
        degp[r // 2, (r % 2) * 4 : (r % 2) * 4 + 4, :] = sums


def step_kernel(
    src, rows, dst_v, rows_v, x_ref, cols, xnear, self1, neigh1, self2, neigh2, nbrs, out,
    plan_v, plan_s, degp, xs, cv, buf, parts, stage, weights, wall, a1, b1, a2, b2, ac, ao, bo, bc, dgot, degx, dz_got,
    zs, zr, near, sums, r2, s3, hs, r3, rh, s4, r4,
    plan_sem, csem, wsem, nsem, xsend, xrecv, dsem, esem, zsend, zrecv, fsem, gsend, grecv, psem,
):
    node, f = lax.axis_index("node"), lax.axis_index("feat")
    x, z = node // NZ, node % NZ
    y, core = f // 2, f % 2
    nf = wall.shape[0]
    xp, xm, xo = (x + 1) % NX, (x + NX - 1) % NX, (x + 2) % NX
    half = a1.shape[1]
    body = 2 * half
    slots, depth = cv.shape[2], cv.shape[3]

    def at(xx=x, zz=z, ff=f):
        return {"node": xx * NZ + zz, "feat": ff}

    def send(source, target, send_sem, recv_sem, device):
        copy = pltpu.make_async_remote_copy(
            src_ref=source, dst_ref=target, send_sem=send_sem, recv_sem=recv_sem,
            device_id=device, device_id_type=MESH,
        )
        copy.start()

    def landed(ref, sem):
        pltpu.make_async_copy(ref, ref, sem).wait()

    def order(i):
        return (4 + (1 - 2 * (i % 2)) * ((i + 1) // 2)) % NZ

    def loop(lo, hi, fn):
        lax.fori_loop(lo, hi, lambda i, c: (fn(i), c)[1], 0)

    barrier = pltpu.get_barrier_semaphore()

    def greet(device):
        pl.semaphore_signal(barrier, inc=1, device_id=device, device_id_type=MESH)

    loop(0, NX - 1, lambda i: greet(at(xx=(x + 1 + i) % NX)))
    loop(0, NZ - 1, lambda i: greet(at(zz=(z + 1 + i) % NZ)))
    loop(0, nf - 1, lambda i: greet(at(ff=(f + 1 + i) % nf)))

    def columns_in(i):
        zi = (z + order(i)) % NZ
        pltpu.make_async_copy(cols.at[:, zi], cv.at[:, zi], csem.at[i]).start()

    loop(0, NZ, columns_in)

    targets = dst_v[...]
    plan_v[0:8], plan_v[8:16] = slot_plan(targets)
    plan_copy = pltpu.make_async_copy(plan_v, plan_s, plan_sem)
    plan_copy.start()
    block_counts(jnp.where(targets == f, rows_v[...], 0), degp)
    for b in range(xs.shape[0]):
        xs[b] = x_ref[:, b * LANES : (b + 1) * LANES].astype(F32)
    buf[...] = jnp.zeros_like(buf)
    for b in range(nf):
        near[b] = xnear[:, b * LANES : (b + 1) * LANES].astype(F32)
    stage[...] = jnp.zeros_like(stage)
    stage[0:8] = self1[...].astype(F32)
    stage[8:16] = neigh1[...].astype(F32)
    stage[16:32, 0 : self2.shape[1]] = self2[...].astype(F32)
    stage[32:48, 0 : neigh2.shape[1]] = neigh2[...].astype(F32)
    weights[...] = stage[...].astype(BF16)
    lane = lax.broadcasted_iota(jnp.int32, (8, LANES), 1)

    rows_of = lax.broadcasted_iota(jnp.int32, (16, LANES), 0)
    ids = [(rows_of + 16 * g).astype(jnp.int16) for g in range(LANES // 16)]
    one, zero = jnp.ones((16, LANES), BF16), jnp.zeros((16, LANES), BF16)

    def gathered(block, xx, zi, s):
        got = []
        for k in range(depth):
            index = jnp.broadcast_to(cv[xx, zi, s, pl.ds(k, 1), :], (8, LANES))
            got.append(jnp.take_along_axis(block, index, axis=1, mode="promise_in_bounds"))
        return functools.reduce(lambda a, b: a + b, got)

    def counted(block, xx, zi, s):
        index = [
            jnp.broadcast_to(cv[xx, zi, s, pl.ds(k, 1), :], (16, LANES)).astype(jnp.int16)
            for k in range(depth)
        ]
        groups = []
        for g in ids:
            hits = [jnp.where(row == g, one, zero) for row in index]
            groups.append(functools.reduce(lambda a, b: a + b, hits))
        matrix = jnp.concatenate(groups, axis=0)
        return jnp.dot(block.astype(BF16), matrix, preferred_element_type=F32)

    def tile_sums(xx, zi):
        target = xx * NZ + zi
        base, line, lane0 = target * slots, target // 4, target % 4 * slots
        for s in range(slots):
            block = xs[src[base + s]]
            total = (counted if s % 8 in (2, 5, 7) else gathered)(block, xx, zi, s)
            buf[s] = jnp.where(lane < rows[base + s], total, 0.0) + buf[plan_s[line, lane0 + s]]
        for b in range(0, nf, 2):
            pair = [buf[plan_s[8 + line, lane0 + b + j]] for j in (0, 1)]
            parts[xx, zi, b * 8 : b * 8 + 16] = jnp.concatenate(pair, axis=0).astype(BF16)

    def first(i):
        zi = (z + order(i)) % NZ
        send(parts.at[xo, zi, pl.ds(0, half)], a1.at[zi], xsend.at[0, zi], xrecv.at[0, zi], at(xx=xp))
        send(parts.at[xo, zi, pl.ds(half, half)], b1.at[zi], xsend.at[1, zi], xrecv.at[1, zi], at(xx=xm))

    def direct_up(i):
        zi = (z + order(i)) % NZ
        send(parts.at[xp, zi, pl.ds(half, half)], bo.at[zi], xsend.at[2, zi], xrecv.at[2, zi], at(xx=xp))

    def direct_down(i):
        zi = (z + order(i)) % NZ
        send(parts.at[xm, zi, pl.ds(0, half)], ao.at[zi], xsend.at[3, zi], xrecv.at[3, zi], at(xx=xm))

    def relay_up(i):
        zi = (z + order(i)) % NZ
        landed(a1.at[zi], xrecv.at[0, zi])
        a2[zi] = (a1[zi].astype(F32) + parts[xp, zi, pl.ds(0, half), :].astype(F32)).astype(BF16)
        send(a2.at[zi], ac.at[zi], xsend.at[4, zi], xrecv.at[4, zi], at(xx=xp))

    def relay_down(i):
        zi = (z + order(i)) % NZ
        landed(b1.at[zi], xrecv.at[1, zi])
        b2[zi] = (b1[zi].astype(F32) + parts[xm, zi, pl.ds(half, half), :].astype(F32)).astype(BF16)
        send(b2.at[zi], bc.at[zi], xsend.at[5, zi], xrecv.at[5, zi], at(xx=xm))

    def summed(i):
        zi = (z + order(i)) % NZ
        for kind, ref in ((2, bo), (3, ao), (4, ac), (5, bc)):
            landed(ref.at[zi], xrecv.at[kind, zi])
        upper = parts[x, zi, pl.ds(0, half), :].astype(F32) + ao[zi].astype(F32) + ac[zi].astype(F32)
        lower = parts[x, zi, pl.ds(half, half), :].astype(F32) + bo[zi].astype(F32) + bc[zi].astype(F32)
        return upper, lower

    def onward(i):
        dz = order(i)
        zi = (z + dz) % NZ
        upper, lower = summed(i)
        zs[dz - 1, 0:half] = upper.astype(BF16)
        zs[dz - 1, half:body] = lower.astype(BF16)
        send(zs.at[dz - 1], zr.at[dz - 1], zsend.at[dz - 1], zrecv.at[dz - 1], at(zz=zi))

    plan_copy.wait()

    def far(i):
        landed(cv.at[:, 0], csem.at[i])
        tile_sums(xo, (z + order(i)) % NZ)

    loop(0, NZ, far)
    pl.semaphore_wait(barrier, NX - 1 + NZ - 1 + nf - 1)
    loop(0, NZ, first)
    for i in range(NX - 1):
        send(degp.at[(x + 1 + i) % NX], dgot.at[i], dsem.at[0, i], dsem.at[1, i], at(xx=(x + 1 + i) % NX))

    wall[f] = weights[...]
    r2[f, 0:8] = near[f]

    def early(i):
        p = (f + 1 + i) % nf
        send(near.at[p], r2.at[f, pl.ds(0, 8)], nsem.at[0, 0], nsem.at[1, f], at(ff=p))
        send(weights, wall.at[f], wsem.at[0], wsem.at[1], at(ff=p))

    loop(0, nf - 1, early)

    lag = 3

    def step(n):
        i, q = n // 3, n % 3
        tile_sums((x + 1 + 2 * q + 3 * (q // 2)) % NX, (z + order(i)) % NZ)

        @pl.when(q == 0)
        def _():
            direct_up(i)
            relay_up(i)

        @pl.when(q == 1)
        def _():
            direct_down(i)
            relay_down(i)

        @pl.when((q == 2) & (i >= lag))
        def _():
            onward(i - lag)

        @pl.when(n == 7)
        def _():
            for j in range(NX - 1):
                landed(dgot.at[j], dsem.at[1, j])
            degx[...] = degp[x] + dgot[0] + dgot[1] + dgot[2]
            for dz in range(1, NZ):
                send(degx, dz_got.at[dz - 1], esem.at[0, dz - 1], esem.at[1, dz - 1], at(zz=(z + dz) % NZ))

    loop(0, 3 * NZ, step)
    loop(NZ - lag, NZ - 1, onward)

    own_nodes = lax.broadcasted_iota(jnp.int32, (LANES, nbrs.shape[1]), 0) + f * LANES
    counts = jnp.zeros(own_nodes.shape, F32)
    for n in range(FAN2):
        counts += jnp.where(nbrs[n : n + 1, :] == own_nodes, 1.0, 0.0)
    counts = jnp.transpose(counts).astype(BF16)
    deg = degx[pl.ds(z, 1), :]
    for i in range(NZ - 1):
        landed(dz_got.at[i], esem.at[1, i])
        deg += dz_got[i, pl.ds(z, 1), :]
    deg = jnp.maximum(4.0 * deg, 1.0)

    upper, lower = summed(NZ - 1)
    for i in (3, 2, 4, 1, 5, 0, 6):
        landed(zr.at[i], zrecv.at[i])
        upper += zr[i, 0:half].astype(F32)
        lower += zr[i, half:body].astype(F32)
    for b in range(nf // 2):
        sums[b] = upper[b * 8 : b * 8 + 8]
        sums[b + nf // 2] = lower[b * 8 : b * 8 + 8]

    def spread(i):
        p = (f + 1 + i) % nf
        send(sums.at[p], r2.at[f, pl.ds(8, 8)], fsem.at[0], fsem.at[1], at(ff=p))

    loop(0, nf - 1, spread)
    r2[f, 8:16] = sums[f]
    landed(wall.at[pl.ds(0, nf - 1)], wsem.at[1])

    def near_in(i):
        p = (f + 1 + i) % nf
        landed(near.at[p], nsem.at[1, p])

    loop(0, nf - 1, near_in)
    landed(sums.at[pl.ds(0, nf - 1)], fsem.at[1])
    both = r2[...].reshape(nf * 16, LANES)
    is_sum = lax.broadcasted_iota(jnp.int32, both.shape, 0) % 16 >= 8
    both = jnp.where(is_sum, both / deg, both).astype(BF16)
    w1 = wall[:, 0:16, :].reshape(nf * 16, wall.shape[2])
    pre = lax.dot_general(both, w1, (((0,), (0,)), ((), ())), preferred_element_type=F32)
    hidden = jnp.maximum(pre, 0.0).astype(BF16)
    seed_sums = jnp.dot(counts, hidden, preferred_element_type=F32)
    for p in range(nf):
        piece = seed_sums[p * 8 : p * 8 + 8]
        s3[p] = jnp.concatenate([piece[:, 0:LANES], piece[:, LANES:]], axis=0).astype(BF16)

    @pl.when(f == 0)
    def _():
        wide = hidden.astype(F32)
        for p in range(nf):
            piece = wide[p * 8 : p * 8 + 8]
            hs[p] = jnp.concatenate([piece[:, 0:LANES], piece[:, LANES:]], axis=0).astype(BF16)

    def seeds_out(i):
        p = (f + 1 + i) % nf
        send(s3.at[p], r3.at[f], fsem.at[2], fsem.at[3], at(ff=p))

        @pl.when(f == 0)
        def _():
            send(hs.at[p], rh, fsem.at[4], fsem.at[5], at(ff=p))

    loop(0, nf - 1, seeds_out)
    r3[f] = s3[f]

    @pl.when(f == 0)
    def _():
        rh[...] = hs[0]

    @pl.when(f != 0)
    def _():
        landed(rh, fsem.at[5])

    w2s = wall[:, 16:32, :].reshape(nf * 16, wall.shape[2])
    w2n = wall[:, 32:48, :].reshape(nf * 16, wall.shape[2])

    def rejoin(v):
        return jnp.concatenate([v[0:8], v[8:16]], axis=1).astype(BF16)

    logits = jnp.dot(rejoin(rh[...].astype(F32)), w2s, preferred_element_type=F32)
    landed(s3.at[pl.ds(0, nf - 1)], fsem.at[3])
    mean = jnp.zeros(r3.shape[1:], F32)
    for p in range(nf):
        mean += r3[p].astype(F32)
    logits += jnp.dot(rejoin(mean / FAN2), w2n, preferred_element_type=F32)

    s4[...] = logits
    other = at(ff=f + 1 - 2 * core)

    def along(i):
        yy = (y + 1 + i) % (nf // 2)
        send(s4, r4.at[core, y], gsend.at[i], grecv.at[y], at(ff=yy * 2 + core))

    loop(0, nf // 2 - 1, along)
    send(s4, r4.at[core, y], gsend.at[nf // 2 - 1], psem.at[1, y], other)
    r4[core, y] = logits

    def across(i):
        yy = (y + nf + (1 - 2 * (i % 2)) * (i // 2 + 1)) % (nf // 2)
        landed(s4, grecv.at[yy])
        send(r4.at[core, yy], r4.at[core, yy], psem.at[0, i], psem.at[1, yy], other)

    loop(0, nf // 2 - 1, across)

    def sent(i):
        for kind, ref in ((0, a1), (1, b1), (2, bo), (3, ao), (4, ac), (5, bc)):
            landed(ref.at[i], xsend.at[kind, i])

    loop(0, NZ, sent)
    for i in range(NX - 1):
        landed(dgot.at[i], dsem.at[0, i])
    for i in range(NZ - 1):
        landed(zr.at[i], zsend.at[i])
        landed(dz_got.at[i], esem.at[0, i])
    landed(wall.at[pl.ds(0, nf - 1)], wsem.at[0])
    landed(near.at[pl.ds(0, nf - 1)], nsem.at[0, 0])
    landed(sums.at[pl.ds(0, nf - 1)], fsem.at[0])
    landed(s3.at[pl.ds(0, nf - 1)], fsem.at[2])

    @pl.when(f == 0)
    def _():
        landed(hs.at[pl.ds(0, nf - 1)], fsem.at[4])

    for i in range(nf // 2):
        landed(s4, gsend.at[i])
        landed(s4, psem.at[1, i])
    for i in range(nf // 2 - 1):
        landed(s4, psem.at[0, i])
    for i in range(nf):
        out[i] = r4[i % 2, i // 2]


def seed_logits(src, dst, rows, x, cols, xnear, w, nbrs, feats):
    self1, neigh1, self2, neigh2 = w
    hid = self1.shape[1]
    seeds = nbrs.shape[1]
    slots, depth = cols.shape[0] // (NX * NZ), cols.shape[1]
    body = feats * 8
    half = body // 2
    vm = pl.BlockSpec(memory_space=pltpu.VMEM)
    sm = pl.BlockSpec(memory_space=pltpu.SMEM)
    quarter = pltpu.VMEM((NZ, half, LANES), BF16)
    dma = pltpu.SemaphoreType.DMA
    return pl.pallas_call(
        step_kernel,
        out_shape=jax.ShapeDtypeStruct((feats, seeds // feats, hid), F32),
        in_specs=[sm] * 2 + [vm] * 3 + [pl.BlockSpec(memory_space=pl.ANY)] + [vm] * 6,
        out_specs=vm,
        scratch_shapes=[
            pltpu.VMEM((16, LANES), jnp.int32),
            pltpu.SMEM((16, LANES), jnp.int32),
            pltpu.VMEM((NX, NZ, LANES), F32),
            pltpu.VMEM((x.shape[1] // LANES, 8, LANES), F32),
            pltpu.VMEM((NX, NZ, slots, depth, LANES), jnp.int32),
            pltpu.VMEM((slots + 1, 8, LANES), F32),
            pltpu.VMEM((NX, NZ, body, LANES), BF16),
            pltpu.VMEM((48, hid), F32),
            pltpu.VMEM((48, hid), BF16),
            pltpu.VMEM((feats, 48, hid), BF16),
            *[quarter] * 8,
            pltpu.VMEM((NX - 1, NZ, LANES), F32),
            pltpu.VMEM((NZ, LANES), F32),
            pltpu.VMEM((NZ - 1, NZ, LANES), F32),
            pltpu.VMEM((NZ - 1, body, LANES), BF16),
            pltpu.VMEM((NZ - 1, body, LANES), BF16),
            pltpu.VMEM((feats, 8, LANES), F32),
            pltpu.VMEM((feats, 8, LANES), F32),
            pltpu.VMEM((feats, 16, LANES), F32),
            pltpu.VMEM((feats, 16, LANES), BF16),
            pltpu.VMEM((feats, 16, LANES), BF16),
            pltpu.VMEM((feats, 16, LANES), BF16),
            pltpu.VMEM((16, LANES), BF16),
            pltpu.VMEM((8, hid), F32),
            pltpu.VMEM((2, feats // 2, 8, hid), F32),
            dma(()),
            dma((NZ,)),
            dma((2,)),
            dma((2, feats)),
            dma((6, NZ)),
            dma((6, NZ)),
            dma((2, NX - 1)),
            dma((2, NZ - 1)),
            dma((NZ - 1,)),
            dma((NZ - 1,)),
            dma((6,)),
            dma((feats // 2,)),
            dma((feats // 2,)),
            dma((2, feats // 2)),
        ],
        compiler_params=pltpu.CompilerParams(
            collective_id=0, has_side_effects=True, vmem_limit_bytes=VMEM
        ),
    )(
        src, rows, dst.reshape(8, LANES), rows.reshape(8, LANES), x,
        cols.reshape(NX, NZ, slots, depth, LANES), xnear, self1, neigh1, self2, neigh2, nbrs,
    )


def loss_kernel(table, labels, logits, loss):
    full = jnp.transpose(table[...])
    rows = full[0 : logits.shape[0]]
    logits[...] = rows
    classes = lax.broadcasted_iota(jnp.int32, rows.shape, 0)
    picked = jnp.sum(jnp.where(classes == labels[...], rows, 0.0), axis=0, keepdims=True)
    loss[...] = jnp.log(jnp.sum(jnp.exp(rows), axis=0, keepdims=True)) - picked


def per_device(
    x_far,
    x_near,
    tile_src,
    tile_dst,
    tile_rows,
    tile_cols,
    seed_nbrs,
    labels,
    self_one,
    neigh_one,
    self_two,
    neigh_two,
):
    feats = lax.axis_size("feat")
    classes, hid = self_two.shape[0], self_one.shape[0]
    seeds = labels.shape[0]
    weights = (self_one.T, neigh_one.T, self_two.T, neigh_two.T)
    table = seed_logits(
        tile_src, tile_dst, tile_rows, x_far, tile_cols, x_near, weights, seed_nbrs.T, feats
    )
    logits, loss = pl.pallas_call(
        loss_kernel,
        out_shape=(
            jax.ShapeDtypeStruct((classes, seeds), F32),
            jax.ShapeDtypeStruct((1, seeds), F32),
        ),
        compiler_params=pltpu.CompilerParams(vmem_limit_bytes=VMEM),
    )(table.reshape(seeds, hid), labels.reshape(1, seeds))
    return logits, loss.reshape(seeds)


def solution(mesh):
    placed = (
        P("feat", "node"),
        P("feat", "node"),
        P("node"),
        P("node"),
        P("node"),
        P("node", None, None),
        P("node", None),
        P("node"),
        P(None, "feat"),
        P(None, "feat"),
        P(None, "feat"),
        P(None, "feat"),
    )
    return jax.shard_map(
        per_device,
        mesh=mesh,
        in_specs=placed,
        out_specs=(P(None, "node"), P("node")),
        check_vma=False,
    )
```

```python
import functools

import jax
import jax.numpy as jnp
from jax import lax
from jax.experimental import pallas as pl
from jax.experimental.pallas import tpu as pltpu
from jax.sharding import PartitionSpec as P

FAN2 = 10
NX, NZ = 4, 8
LANES = 128
VMEM = 60 * 1024 * 1024
MESH = pl.DeviceIdType.MESH
F32, BF16 = jnp.float32, jnp.bfloat16


def slot_plan(d):
    slots = 32
    pos = lax.broadcasted_iota(jnp.int32, d.shape, 1) % slots
    prev = jnp.full(d.shape, slots, jnp.int32)
    for s in range(slots - 1, 0, -1):
        prev = jnp.where((pos >= s) & (pltpu.roll(d, s, 1) == d), pos - s, prev)
    last = jnp.full(d.shape, slots, jnp.int32)
    for b in range(16):
        v = jnp.where(d == b, pos, -1)
        for s in (1, 2, 4, 8, 16):
            v = jnp.maximum(v, jnp.where((pos & s) == 0, pltpu.roll(v, LANES - s, 1), pltpu.roll(v, s, 1)))
        last = jnp.where((pos == b) & (v >= 0), v, last)
    return prev, last


def block_counts(rows, degp):
    columns = jnp.transpose(jnp.concatenate([rows.astype(F32)] * 16, axis=0))
    across = lax.broadcasted_iota(jnp.int32, (LANES, LANES), 1).astype(F32)
    for r in range(8):
        live = jnp.where(across < columns[:, r : r + 1], 1.0, 0.0)
        sums = jnp.sum(live.reshape(4, LANES // 4, LANES), axis=1)
        degp[r // 2, (r % 2) * 4 : (r % 2) * 4 + 4, :] = sums


def step_kernel(
    src, rows, dst_v, rows_v, x_ref, cols, xnear, self1, neigh1, self2, neigh2, nbrs, out,
    plan_v, plan_s, degp, xs, cv, buf, parts, stage, weights, wall, a1, b1, a2, b2, ac, ao, bo, bc, dgot, degx, dz_got,
    zs, zr, picks, w1t, near, sums, r2, s3, hs, r3, rh, s4, r4,
    plan_sem, csem, wsem, nsem, xsend, xrecv, dsem, esem, zsend, zrecv, fsem, gsend, grecv, psem,
):
    node, f = lax.axis_index("node"), lax.axis_index("feat")
    x, z = node // NZ, node % NZ
    y, core = f // 2, f % 2
    nf = wall.shape[0]
    xp, xm, xo = (x + 1) % NX, (x + NX - 1) % NX, (x + 2) % NX
    half = a1.shape[1]
    body = 2 * half
    slots, depth = cv.shape[2], cv.shape[3]

    def at(xx=x, zz=z, ff=f):
        return {"node": xx * NZ + zz, "feat": ff}

    def send(source, target, send_sem, recv_sem, device):
        copy = pltpu.make_async_remote_copy(
            src_ref=source, dst_ref=target, send_sem=send_sem, recv_sem=recv_sem,
            device_id=device, device_id_type=MESH,
        )
        copy.start()

    def landed(ref, sem):
        pltpu.make_async_copy(ref, ref, sem).wait()

    def order(i):
        return (4 + (1 - 2 * (i % 2)) * ((i + 1) // 2)) % NZ

    def loop(lo, hi, fn):
        lax.fori_loop(lo, hi, lambda i, c: (fn(i), c)[1], 0)

    barrier = pltpu.get_barrier_semaphore()

    def greet(device):
        pl.semaphore_signal(barrier, inc=1, device_id=device, device_id_type=MESH)

    loop(0, NX - 1, lambda i: greet(at(xx=(x + 1 + i) % NX)))
    loop(0, NZ - 1, lambda i: greet(at(zz=(z + 1 + i) % NZ)))
    loop(0, nf - 1, lambda i: greet(at(ff=(f + 1 + i) % nf)))

    def columns_in(i):
        zi = (z + order(i)) % NZ
        pltpu.make_async_copy(cols.at[:, zi], cv.at[:, zi], csem.at[i]).start()

    loop(0, NZ, columns_in)

    plan_v[0:8], plan_v[8:16] = slot_plan(dst_v[...])
    plan_copy = pltpu.make_async_copy(plan_v, plan_s, plan_sem)
    plan_copy.start()
    for b in range(xs.shape[0]):
        xs[b] = x_ref[:, b * LANES : (b + 1) * LANES].astype(F32)
    buf[...] = jnp.zeros_like(buf)
    for b in range(nf):
        near[b] = xnear[:, b * LANES : (b + 1) * LANES].astype(F32)
    stage[...] = jnp.zeros_like(stage)
    stage[0:8] = self1[...].astype(F32)
    stage[8:16] = neigh1[...].astype(F32)
    stage[16:32, 0 : self2.shape[1]] = self2[...].astype(F32)
    stage[32:48, 0 : neigh2.shape[1]] = neigh2[...].astype(F32)
    weights[...] = stage[...].astype(BF16)
    lane = lax.broadcasted_iota(jnp.int32, (8, LANES), 1)

    rows_of = lax.broadcasted_iota(jnp.int32, (16, LANES), 0)
    ids = [(rows_of + 16 * g).astype(jnp.int16) for g in range(LANES // 16)]
    one, zero = jnp.ones((16, LANES), BF16), jnp.zeros((16, LANES), BF16)

    def gathered(block, xx, zi, s):
        got = []
        for k in range(depth):
            index = jnp.broadcast_to(cv[xx, zi, s, pl.ds(k, 1), :], (8, LANES))
            got.append(jnp.take_along_axis(block, index, axis=1, mode="promise_in_bounds"))
        return functools.reduce(lambda a, b: a + b, got)

    def counted(block, xx, zi, s):
        index = [
            jnp.broadcast_to(cv[xx, zi, s, pl.ds(k, 1), :], (16, LANES)).astype(jnp.int16)
            for k in range(depth)
        ]
        groups = []
        for g in ids:
            hits = [jnp.where(row == g, one, zero) for row in index]
            groups.append(functools.reduce(lambda a, b: a + b, hits))
        matrix = jnp.concatenate(groups, axis=0)
        return jnp.dot(block.astype(BF16), matrix, preferred_element_type=F32)

    def tile_sums(xx, zi):
        target = xx * NZ + zi
        base, line, lane0 = target * slots, target // 4, target % 4 * slots
        for s in range(slots):
            block = xs[src[base + s]]
            total = (counted if s % 8 in (2, 5, 7) else gathered)(block, xx, zi, s)
            buf[s] = jnp.where(lane < rows[base + s], total, 0.0) + buf[plan_s[line, lane0 + s]]
        for b in range(0, nf, 2):
            pair = [buf[plan_s[8 + line, lane0 + b + j]] for j in (0, 1)]
            parts[xx, zi, b * 8 : b * 8 + 16] = jnp.concatenate(pair, axis=0).astype(BF16)

    def first(i):
        zi = (z + order(i)) % NZ
        send(parts.at[xo, zi, pl.ds(0, half)], a1.at[zi], xsend.at[0, zi], xrecv.at[0, zi], at(xx=xp))
        send(parts.at[xo, zi, pl.ds(half, half)], b1.at[zi], xsend.at[1, zi], xrecv.at[1, zi], at(xx=xm))

    def direct_up(i):
        zi = (z + order(i)) % NZ
        send(parts.at[xp, zi, pl.ds(half, half)], bo.at[zi], xsend.at[2, zi], xrecv.at[2, zi], at(xx=xp))

    def direct_down(i):
        zi = (z + order(i)) % NZ
        send(parts.at[xm, zi, pl.ds(0, half)], ao.at[zi], xsend.at[3, zi], xrecv.at[3, zi], at(xx=xm))

    def relay_up(i):
        zi = (z + order(i)) % NZ
        landed(a1.at[zi], xrecv.at[0, zi])
        a2[zi] = (a1[zi].astype(F32) + parts[xp, zi, pl.ds(0, half), :].astype(F32)).astype(BF16)
        send(a2.at[zi], ac.at[zi], xsend.at[4, zi], xrecv.at[4, zi], at(xx=xp))

    def relay_down(i):
        zi = (z + order(i)) % NZ
        landed(b1.at[zi], xrecv.at[1, zi])
        b2[zi] = (b1[zi].astype(F32) + parts[xm, zi, pl.ds(half, half), :].astype(F32)).astype(BF16)
        send(b2.at[zi], bc.at[zi], xsend.at[5, zi], xrecv.at[5, zi], at(xx=xm))

    def summed(i):
        zi = (z + order(i)) % NZ
        for kind, ref in ((2, bo), (3, ao), (4, ac), (5, bc)):
            landed(ref.at[zi], xrecv.at[kind, zi])
        upper = parts[x, zi, pl.ds(0, half), :].astype(F32) + ao[zi].astype(F32) + ac[zi].astype(F32)
        lower = parts[x, zi, pl.ds(half, half), :].astype(F32) + bo[zi].astype(F32) + bc[zi].astype(F32)
        return upper, lower

    def onward(i):
        dz = order(i)
        zi = (z + dz) % NZ
        upper, lower = summed(i)
        zs[dz - 1, 0:half] = upper.astype(BF16)
        zs[dz - 1, half:body] = lower.astype(BF16)
        send(zs.at[dz - 1], zr.at[dz - 1], zsend.at[dz - 1], zrecv.at[dz - 1], at(zz=zi))

    plan_copy.wait()

    def own_x(i):
        landed(cv.at[:, 0], csem.at[i])
        tile_sums(x, (z + order(i)) % NZ)

    loop(0, NZ, own_x)
    wall[f] = weights[...]
    r2[f, 0:8] = near[f]
    pl.semaphore_wait(barrier, NX - 1 + NZ - 1 + nf - 1)

    def early(i):
        p = (f + 1 + i) % nf
        send(near.at[p], r2.at[f, pl.ds(0, 8)], nsem.at[0, 0], nsem.at[1, f], at(ff=p))
        send(weights, wall.at[f], wsem.at[0], wsem.at[1], at(ff=p))

    def far(i):
        early(i)
        tile_sums(xo, (z + order(i)) % NZ)
        first(i)

    loop(0, NZ, far)
    onward_lag = 4

    def beside(i):
        zi = (z + order(i)) % NZ

        @pl.when(i < nf - 1 - NZ)
        def _():
            early(NZ + i)

        tile_sums(xp, zi)
        direct_up(i)
        relay_up(i)
        tile_sums(xm, zi)
        direct_down(i)
        relay_down(i)

        @pl.when(i >= onward_lag)
        def _():
            onward(i - onward_lag)

    loop(0, NZ, beside)

    block_counts(jnp.where(dst_v[...] == f, rows_v[...], 0), degp)
    for i in range(NX - 1):
        send(degp.at[(x + 1 + i) % NX], dgot.at[i], dsem.at[0, i], dsem.at[1, i], at(xx=(x + 1 + i) % NX))
    loop(NZ - onward_lag, NZ - 1, onward)
    for i in range(NX - 1):
        landed(dgot.at[i], dsem.at[1, i])
    degx[...] = degp[x] + dgot[0] + dgot[1] + dgot[2]
    for dz in range(1, NZ):
        send(degx, dz_got.at[dz - 1], esem.at[0, dz - 1], esem.at[1, dz - 1], at(zz=(z + dz) % NZ))

    own_nodes = lax.broadcasted_iota(jnp.int32, (LANES, nbrs.shape[1]), 0) + f * LANES
    counts = jnp.zeros(own_nodes.shape, F32)
    for n in range(FAN2):
        counts += jnp.where(nbrs[n : n + 1, :] == own_nodes, 1.0, 0.0)
    picks[...] = jnp.transpose(counts).astype(BF16)
    landed(wall.at[pl.ds(0, nf - 1)], wsem.at[1])
    w1 = wall[:, 0:16, :].reshape(nf * 16, wall.shape[2])
    w1t[...] = jnp.transpose(w1.astype(F32)).astype(BF16)

    upper, lower = summed(NZ - 1)
    for i in (3, 2, 4, 1, 5, 0, 6):
        landed(zr.at[i], zrecv.at[i])
        upper += zr[i, 0:half].astype(F32)
        lower += zr[i, half:body].astype(F32)
    for b in range(nf // 2):
        sums[b] = upper[b * 8 : b * 8 + 8]
        sums[b + nf // 2] = lower[b * 8 : b * 8 + 8]

    def spread(i):
        p = (f + 1 + i) % nf
        send(sums.at[p], r2.at[f, pl.ds(8, 8)], fsem.at[0], fsem.at[1], at(ff=p))

    loop(0, nf - 1, spread)
    r2[f, 8:16] = sums[f]
    deg = degx[pl.ds(z, 1), :]
    for i in range(NZ - 1):
        landed(dz_got.at[i], esem.at[1, i])
        deg += dz_got[i, pl.ds(z, 1), :]
    scale = 1.0 / jnp.maximum(4.0 * deg, 1.0)

    def near_in(i):
        p = (f + 1 + i) % nf
        landed(near.at[p], nsem.at[1, p])

    loop(0, nf - 1, near_in)
    landed(sums.at[pl.ds(0, nf - 1)], fsem.at[1])
    both = r2[...].reshape(nf * 16, LANES)
    is_sum = lax.broadcasted_iota(jnp.int32, both.shape, 0) % 16 >= 8
    both = jnp.where(is_sum, both * scale, both).astype(BF16)
    hidden = jnp.maximum(jnp.dot(w1t[...], both, preferred_element_type=F32), 0.0).astype(BF16)
    across = (((1,), (1,)), ((), ()))
    seed_sums = lax.dot_general(picks[...], hidden, across, preferred_element_type=F32)
    for p in range(nf):
        piece = seed_sums[p * 8 : p * 8 + 8]
        s3[p] = jnp.concatenate([piece[:, 0:LANES], piece[:, LANES:]], axis=0).astype(BF16)

    @pl.when(f == 0)
    def _():
        diagonal = lax.broadcasted_iota(jnp.int32, (LANES, LANES), 0) == lax.broadcasted_iota(
            jnp.int32, (LANES, LANES), 1
        )
        wide = lax.dot_general(
            jnp.where(diagonal, 1.0, 0.0).astype(BF16), hidden, across, preferred_element_type=F32
        )
        for p in range(nf):
            piece = wide[p * 8 : p * 8 + 8]
            hs[p] = jnp.concatenate([piece[:, 0:LANES], piece[:, LANES:]], axis=0).astype(BF16)

    def seeds_out(i):
        p = (f + 1 + i) % nf
        send(s3.at[p], r3.at[f], fsem.at[2], fsem.at[3], at(ff=p))

        @pl.when(f == 0)
        def _():
            send(hs.at[p], rh, fsem.at[4], fsem.at[5], at(ff=p))

    loop(0, nf - 1, seeds_out)
    r3[f] = s3[f]

    @pl.when(f == 0)
    def _():
        rh[...] = hs[0]

    @pl.when(f != 0)
    def _():
        landed(rh, fsem.at[5])

    w2s = wall[:, 16:32, :].reshape(nf * 16, wall.shape[2])
    w2n = wall[:, 32:48, :].reshape(nf * 16, wall.shape[2])

    def rejoin(v):
        return jnp.concatenate([v[0:8], v[8:16]], axis=1).astype(BF16)

    logits = jnp.dot(rejoin(rh[...].astype(F32)), w2s, preferred_element_type=F32)
    landed(s3.at[pl.ds(0, nf - 1)], fsem.at[3])
    mean = jnp.zeros(r3.shape[1:], F32)
    for p in range(nf):
        mean += r3[p].astype(F32)
    logits += jnp.dot(rejoin(mean / FAN2), w2n, preferred_element_type=F32)

    s4[...] = logits
    other = at(ff=f + 1 - 2 * core)

    def along(i):
        yy = (y + 1 + i) % (nf // 2)
        send(s4, r4.at[core, y], gsend.at[i], grecv.at[y], at(ff=yy * 2 + core))

    loop(0, nf // 2 - 1, along)
    send(s4, r4.at[core, y], gsend.at[nf // 2 - 1], psem.at[1, y], other)
    r4[core, y] = logits

    def onto(i):
        yy = (y + nf + (1 - 2 * (i % 2)) * (i // 2 + 1)) % (nf // 2)
        landed(s4, grecv.at[yy])
        send(r4.at[core, yy], r4.at[core, yy], psem.at[0, i], psem.at[1, yy], other)

    loop(0, nf // 2 - 1, onto)

    def sent(i):
        for kind, ref in ((0, a1), (1, b1), (2, bo), (3, ao), (4, ac), (5, bc)):
            landed(ref.at[i], xsend.at[kind, i])

    loop(0, NZ, sent)
    for i in range(NX - 1):
        landed(dgot.at[i], dsem.at[0, i])
    for i in range(NZ - 1):
        landed(zr.at[i], zsend.at[i])
        landed(dz_got.at[i], esem.at[0, i])
    landed(wall.at[pl.ds(0, nf - 1)], wsem.at[0])
    landed(near.at[pl.ds(0, nf - 1)], nsem.at[0, 0])
    landed(sums.at[pl.ds(0, nf - 1)], fsem.at[0])
    landed(s3.at[pl.ds(0, nf - 1)], fsem.at[2])

    @pl.when(f == 0)
    def _():
        landed(hs.at[pl.ds(0, nf - 1)], fsem.at[4])

    for i in range(nf // 2):
        landed(s4, gsend.at[i])
        landed(s4, psem.at[1, i])
    for i in range(nf // 2 - 1):
        landed(s4, psem.at[0, i])
    for i in range(nf):
        out[i] = r4[i % 2, i // 2]


def seed_logits(src, dst, rows, x, cols, xnear, w, nbrs, feats):
    self1, neigh1, self2, neigh2 = w
    hid = self1.shape[1]
    seeds = nbrs.shape[1]
    slots, depth = cols.shape[0] // (NX * NZ), cols.shape[1]
    body = feats * 8
    half = body // 2
    vm = pl.BlockSpec(memory_space=pltpu.VMEM)
    sm = pl.BlockSpec(memory_space=pltpu.SMEM)
    quarter = pltpu.VMEM((NZ, half, LANES), BF16)
    dma = pltpu.SemaphoreType.DMA
    return pl.pallas_call(
        step_kernel,
        out_shape=jax.ShapeDtypeStruct((feats, seeds // feats, hid), F32),
        in_specs=[sm] * 2 + [vm] * 3 + [pl.BlockSpec(memory_space=pl.ANY)] + [vm] * 6,
        out_specs=vm,
        scratch_shapes=[
            pltpu.VMEM((16, LANES), jnp.int32),
            pltpu.SMEM((16, LANES), jnp.int32),
            pltpu.VMEM((NX, NZ, LANES), F32),
            pltpu.VMEM((x.shape[1] // LANES, 8, LANES), F32),
            pltpu.VMEM((NX, NZ, slots, depth, LANES), jnp.int32),
            pltpu.VMEM((slots + 1, 8, LANES), F32),
            pltpu.VMEM((NX, NZ, body, LANES), BF16),
            pltpu.VMEM((48, hid), F32),
            pltpu.VMEM((48, hid), BF16),
            pltpu.VMEM((feats, 48, hid), BF16),
            *[quarter] * 8,
            pltpu.VMEM((NX - 1, NZ, LANES), F32),
            pltpu.VMEM((NZ, LANES), F32),
            pltpu.VMEM((NZ - 1, NZ, LANES), F32),
            pltpu.VMEM((NZ - 1, body, LANES), BF16),
            pltpu.VMEM((NZ - 1, body, LANES), BF16),
            pltpu.VMEM((seeds, LANES), BF16),
            pltpu.VMEM((hid, feats * 16), BF16),
            pltpu.VMEM((feats, 8, LANES), F32),
            pltpu.VMEM((feats, 8, LANES), F32),
            pltpu.VMEM((feats, 16, LANES), F32),
            pltpu.VMEM((feats, 16, LANES), BF16),
            pltpu.VMEM((feats, 16, LANES), BF16),
            pltpu.VMEM((feats, 16, LANES), BF16),
            pltpu.VMEM((16, LANES), BF16),
            pltpu.VMEM((8, hid), F32),
            pltpu.VMEM((2, feats // 2, 8, hid), F32),
            dma(()),
            dma((NZ,)),
            dma((2,)),
            dma((2, feats)),
            dma((6, NZ)),
            dma((6, NZ)),
            dma((2, NX - 1)),
            dma((2, NZ - 1)),
            dma((NZ - 1,)),
            dma((NZ - 1,)),
            dma((6,)),
            dma((feats // 2,)),
            dma((feats // 2,)),
            dma((2, feats // 2)),
        ],
        compiler_params=pltpu.CompilerParams(
            collective_id=0, has_side_effects=True, vmem_limit_bytes=VMEM
        ),
    )(
        src, rows, dst.reshape(8, LANES), rows.reshape(8, LANES), x,
        cols.reshape(NX, NZ, slots, depth, LANES), xnear, self1, neigh1, self2, neigh2, nbrs,
    )


def loss_kernel(table, labels, logits, loss):
    full = jnp.transpose(table[...])
    rows = full[0 : logits.shape[0]]
    logits[...] = rows
    classes = lax.broadcasted_iota(jnp.int32, rows.shape, 0)
    picked = jnp.sum(jnp.where(classes == labels[...], rows, 0.0), axis=0, keepdims=True)
    loss[...] = jnp.log(jnp.sum(jnp.exp(rows), axis=0, keepdims=True)) - picked


def per_device(
    x_far,
    x_near,
    tile_src,
    tile_dst,
    tile_rows,
    tile_cols,
    seed_nbrs,
    labels,
    self_one,
    neigh_one,
    self_two,
    neigh_two,
):
    feats = lax.axis_size("feat")
    classes, hid = self_two.shape[0], self_one.shape[0]
    seeds = labels.shape[0]
    weights = (self_one.T, neigh_one.T, self_two.T, neigh_two.T)
    table = seed_logits(
        tile_src, tile_dst, tile_rows, x_far, tile_cols, x_near, weights, seed_nbrs.T, feats
    )
    logits, loss = pl.pallas_call(
        loss_kernel,
        out_shape=(
            jax.ShapeDtypeStruct((classes, seeds), F32),
            jax.ShapeDtypeStruct((1, seeds), F32),
        ),
        compiler_params=pltpu.CompilerParams(vmem_limit_bytes=VMEM),
    )(table.reshape(seeds, hid), labels.reshape(1, seeds))
    return logits, loss.reshape(seeds)


def solution(mesh):
    placed = (
        P("feat", "node"),
        P("feat", "node"),
        P("node"),
        P("node"),
        P("node"),
        P("node", None, None),
        P("node", None),
        P("node"),
        P(None, "feat"),
        P(None, "feat"),
        P(None, "feat"),
        P(None, "feat"),
    )
    return jax.shard_map(
        per_device,
        mesh=mesh,
        in_specs=placed,
        out_specs=(P(None, "node"), P("node")),
        check_vma=False,
    )
```

```python
import functools

import jax
import jax.numpy as jnp
from jax import lax
from jax.experimental import pallas as pl
from jax.experimental.pallas import tpu as pltpu
from jax.sharding import PartitionSpec as P

FAN2 = 10
NX, NZ = 4, 8
LANES = 128
VMEM = 60 * 1024 * 1024
MESH = pl.DeviceIdType.MESH
F32, BF16 = jnp.float32, jnp.bfloat16


def slot_plan(d):
    slots = 32
    pos = lax.broadcasted_iota(jnp.int32, d.shape, 1) % slots
    prev = jnp.full(d.shape, slots, jnp.int32)
    for s in range(slots - 1, 0, -1):
        prev = jnp.where((pos >= s) & (pltpu.roll(d, s, 1) == d), pos - s, prev)
    last = jnp.full(d.shape, slots, jnp.int32)
    for b in range(16):
        v = jnp.where(d == b, pos, -1)
        for s in (1, 2, 4, 8, 16):
            v = jnp.maximum(v, jnp.where((pos & s) == 0, pltpu.roll(v, LANES - s, 1), pltpu.roll(v, s, 1)))
        last = jnp.where((pos == b) & (v >= 0), v, last)
    return prev, last


def block_counts(rows, degp):
    columns = jnp.transpose(jnp.concatenate([rows.astype(F32)] * 16, axis=0))
    across = lax.broadcasted_iota(jnp.int32, (LANES, LANES), 1).astype(F32)
    for r in range(8):
        live = jnp.where(across < columns[:, r : r + 1], 1.0, 0.0)
        sums = jnp.sum(live.reshape(4, LANES // 4, LANES), axis=1)
        degp[r // 2, (r % 2) * 4 : (r % 2) * 4 + 4, :] = sums


def step_kernel(
    src, rows, dst_v, rows_v, x_ref, cols, xnear, self1, neigh1, self2, neigh2, nbrs, out,
    plan_v, plan_s, degp, xs, cv, buf, parts, stage, weights, wall, a1, b1, a2, b2, ac, ao, bo, bc, dgot, degx, dz_got,
    zs, zr, picks, w1t, near, sums, r2, s3, hs, r3, rh, s4, r4,
    plan_sem, csem, wsem, nsem, xsend, xrecv, dsem, esem, zsend, zrecv, fsem, gsend, grecv, psem,
):
    node, f = lax.axis_index("node"), lax.axis_index("feat")
    x, z = node // NZ, node % NZ
    y, core = f // 2, f % 2
    nf = wall.shape[0]
    xp, xm, xo = (x + 1) % NX, (x + NX - 1) % NX, (x + 2) % NX
    half = a1.shape[1]
    body = 2 * half
    slots, depth = cv.shape[2], cv.shape[3]

    def at(xx=x, zz=z, ff=f):
        return {"node": xx * NZ + zz, "feat": ff}

    def send(source, target, send_sem, recv_sem, device):
        copy = pltpu.make_async_remote_copy(
            src_ref=source, dst_ref=target, send_sem=send_sem, recv_sem=recv_sem,
            device_id=device, device_id_type=MESH,
        )
        copy.start()

    def landed(ref, sem):
        pltpu.make_async_copy(ref, ref, sem).wait()

    def order(i):
        return (4 + (1 - 2 * (i % 2)) * ((i + 1) // 2)) % NZ

    def peer(i):
        return (f + nf // 2 + (1 - 2 * (i % 2)) * ((i + 1) // 2)) % nf

    def loop(lo, hi, fn):
        lax.fori_loop(lo, hi, lambda i, c: (fn(i), c)[1], 0)

    barrier = pltpu.get_barrier_semaphore()

    def greet(device):
        pl.semaphore_signal(barrier, inc=1, device_id=device, device_id_type=MESH)

    loop(0, NX - 1, lambda i: greet(at(xx=(x + 1 + i) % NX)))
    loop(0, NZ - 1, lambda i: greet(at(zz=(z + 1 + i) % NZ)))
    loop(0, nf - 1, lambda i: greet(at(ff=(f + 1 + i) % nf)))

    def columns_in(i):
        zi = (z + order(i)) % NZ
        pltpu.make_async_copy(cols.at[:, zi], cv.at[:, zi], csem.at[i]).start()

    loop(0, NZ, columns_in)

    plan_v[0:8], plan_v[8:16] = slot_plan(dst_v[...])
    plan_copy = pltpu.make_async_copy(plan_v, plan_s, plan_sem)
    plan_copy.start()
    for b in range(xs.shape[0]):
        xs[b] = x_ref[:, b * LANES : (b + 1) * LANES].astype(F32)
    buf[...] = jnp.zeros_like(buf)
    for b in range(nf):
        near[b] = xnear[:, b * LANES : (b + 1) * LANES].astype(F32)
    stage[...] = jnp.zeros_like(stage)
    stage[0:8] = self1[...].astype(F32)
    stage[8:16] = neigh1[...].astype(F32)
    stage[16:32, 0 : self2.shape[1]] = self2[...].astype(F32)
    stage[32:48, 0 : neigh2.shape[1]] = neigh2[...].astype(F32)
    weights[...] = stage[...].astype(BF16)
    lane = lax.broadcasted_iota(jnp.int32, (8, LANES), 1)

    rows_of = lax.broadcasted_iota(jnp.int32, (16, LANES), 0)
    ids = [(rows_of + 16 * g).astype(jnp.int16) for g in range(LANES // 16)]
    one, zero = jnp.ones((16, LANES), BF16), jnp.zeros((16, LANES), BF16)

    def gathered(block, xx, zi, s):
        got = []
        for k in range(depth):
            index = jnp.broadcast_to(cv[xx, zi, s, pl.ds(k, 1), :], (8, LANES))
            got.append(jnp.take_along_axis(block, index, axis=1, mode="promise_in_bounds"))
        return functools.reduce(lambda a, b: a + b, got)

    def counted(block, xx, zi, s):
        index = [
            jnp.broadcast_to(cv[xx, zi, s, pl.ds(k, 1), :], (16, LANES)).astype(jnp.int16)
            for k in range(depth)
        ]
        groups = []
        for g in ids:
            hits = [jnp.where(row == g, one, zero) for row in index]
            groups.append(functools.reduce(lambda a, b: a + b, hits))
        matrix = jnp.concatenate(groups, axis=0)
        return jnp.dot(block.astype(BF16), matrix, preferred_element_type=F32)

    def tile_sums(xx, zi):
        target = xx * NZ + zi
        base, line, lane0 = target * slots, target // 4, target % 4 * slots
        for s in range(slots):
            block = xs[src[base + s]]
            total = (counted if s % 8 in (2, 5, 7) else gathered)(block, xx, zi, s)
            buf[s] = jnp.where(lane < rows[base + s], total, 0.0) + buf[plan_s[line, lane0 + s]]
        for b in range(0, nf, 2):
            pair = [buf[plan_s[8 + line, lane0 + b + j]] for j in (0, 1)]
            parts[xx, zi, b * 8 : b * 8 + 16] = jnp.concatenate(pair, axis=0).astype(BF16)

    def first(i):
        zi = (z + order(i)) % NZ
        send(parts.at[xo, zi, pl.ds(0, half)], a1.at[zi], xsend.at[0, zi], xrecv.at[0, zi], at(xx=xp))
        send(parts.at[xo, zi, pl.ds(half, half)], b1.at[zi], xsend.at[1, zi], xrecv.at[1, zi], at(xx=xm))

    def direct_up(i):
        zi = (z + order(i)) % NZ
        send(parts.at[xp, zi, pl.ds(half, half)], bo.at[zi], xsend.at[2, zi], xrecv.at[2, zi], at(xx=xp))

    def direct_down(i):
        zi = (z + order(i)) % NZ
        send(parts.at[xm, zi, pl.ds(0, half)], ao.at[zi], xsend.at[3, zi], xrecv.at[3, zi], at(xx=xm))

    def relay_up(i):
        zi = (z + order(i)) % NZ
        landed(a1.at[zi], xrecv.at[0, zi])
        a2[zi] = (a1[zi].astype(F32) + parts[xp, zi, pl.ds(0, half), :].astype(F32)).astype(BF16)
        send(a2.at[zi], ac.at[zi], xsend.at[4, zi], xrecv.at[4, zi], at(xx=xp))

    def relay_down(i):
        zi = (z + order(i)) % NZ
        landed(b1.at[zi], xrecv.at[1, zi])
        b2[zi] = (b1[zi].astype(F32) + parts[xm, zi, pl.ds(half, half), :].astype(F32)).astype(BF16)
        send(b2.at[zi], bc.at[zi], xsend.at[5, zi], xrecv.at[5, zi], at(xx=xm))

    def summed(i):
        zi = (z + order(i)) % NZ
        for kind, ref in ((2, bo), (3, ao), (4, ac), (5, bc)):
            landed(ref.at[zi], xrecv.at[kind, zi])
        upper = parts[x, zi, pl.ds(0, half), :].astype(F32) + ao[zi].astype(F32) + ac[zi].astype(F32)
        lower = parts[x, zi, pl.ds(half, half), :].astype(F32) + bo[zi].astype(F32) + bc[zi].astype(F32)
        return upper, lower

    def onward(i):
        dz = order(i)
        zi = (z + dz) % NZ
        upper, lower = summed(i)
        zs[dz - 1, 0:half] = upper.astype(BF16)
        zs[dz - 1, half:body] = lower.astype(BF16)
        send(zs.at[dz - 1], zr.at[dz - 1], zsend.at[dz - 1], zrecv.at[dz - 1], at(zz=zi))

    plan_copy.wait()

    wall[f] = weights[...]
    r2[f, 0:8] = near[f]

    def early(i):
        p = peer(i)
        send(near.at[p], r2.at[f, pl.ds(0, 8)], nsem.at[0, 0], nsem.at[1, f], at(ff=p))
        send(weights, wall.at[f], wsem.at[0], wsem.at[1], at(ff=p))

    def far(i):
        landed(cv.at[:, 0], csem.at[i])
        tile_sums(xo, (z + order(i)) % NZ)

    ahead = 1
    loop(0, ahead, far)
    pl.semaphore_wait(barrier, NX - 1 + NZ - 1 + nf - 1)
    loop(0, ahead, first)

    def far_out(i):
        far(i)
        first(i)

    loop(ahead, NZ, far_out)
    onward_lag = 3

    def beside(i):
        zi = (z + order(i)) % NZ
        early(i)
        tile_sums(xp, zi)
        direct_up(i)
        relay_up(i)
        tile_sums(xm, zi)
        direct_down(i)
        relay_down(i)

        @pl.when(i < nf - 1 - NZ)
        def _():
            early(NZ + i)

        tile_sums(x, zi)

        @pl.when(i >= onward_lag)
        def _():
            onward(i - onward_lag)

    loop(0, NZ, beside)

    block_counts(jnp.where(dst_v[...] == f, rows_v[...], 0), degp)
    for i in range(NX - 1):
        send(degp.at[(x + 1 + i) % NX], dgot.at[i], dsem.at[0, i], dsem.at[1, i], at(xx=(x + 1 + i) % NX))
    loop(NZ - onward_lag, NZ - 1, onward)
    for i in range(NX - 1):
        landed(dgot.at[i], dsem.at[1, i])
    degx[...] = degp[x] + dgot[0] + dgot[1] + dgot[2]
    for dz in range(1, NZ):
        send(degx, dz_got.at[dz - 1], esem.at[0, dz - 1], esem.at[1, dz - 1], at(zz=(z + dz) % NZ))

    own_nodes = lax.broadcasted_iota(jnp.int32, (LANES, nbrs.shape[1]), 0) + f * LANES
    counts = jnp.zeros(own_nodes.shape, F32)
    for n in range(FAN2):
        counts += jnp.where(nbrs[n : n + 1, :] == own_nodes, 1.0, 0.0)
    picks[...] = jnp.transpose(counts).astype(BF16)
    landed(wall.at[pl.ds(0, nf - 1)], wsem.at[1])
    w1 = wall[:, 0:16, :].reshape(nf * 16, wall.shape[2])
    w1t[...] = jnp.transpose(w1.astype(F32)).astype(BF16)

    upper, lower = summed(NZ - 1)
    for i in (3, 2, 4, 1, 5, 0, 6):
        landed(zr.at[i], zrecv.at[i])
        upper += zr[i, 0:half].astype(F32)
        lower += zr[i, half:body].astype(F32)
    for b in range(nf // 2):
        sums[b] = upper[b * 8 : b * 8 + 8]
        sums[b + nf // 2] = lower[b * 8 : b * 8 + 8]

    def spread(i):
        p = peer(i)
        send(sums.at[p], r2.at[f, pl.ds(8, 8)], fsem.at[0], fsem.at[1], at(ff=p))

    loop(0, nf - 1, spread)
    r2[f, 8:16] = sums[f]
    deg = degx[pl.ds(z, 1), :]
    for i in range(NZ - 1):
        landed(dz_got.at[i], esem.at[1, i])
        deg += dz_got[i, pl.ds(z, 1), :]
    scale = 1.0 / jnp.maximum(4.0 * deg, 1.0)

    def near_in(i):
        p = (f + 1 + i) % nf
        landed(near.at[p], nsem.at[1, p])

    loop(0, nf - 1, near_in)
    landed(sums.at[pl.ds(0, nf - 1)], fsem.at[1])
    both = r2[...].reshape(nf * 16, LANES)
    is_sum = lax.broadcasted_iota(jnp.int32, both.shape, 0) % 16 >= 8
    both = jnp.where(is_sum, both * scale, both).astype(BF16)
    hidden = jnp.maximum(jnp.dot(w1t[...], both, preferred_element_type=F32), 0.0).astype(BF16)
    across = (((1,), (1,)), ((), ()))
    seed_sums = lax.dot_general(picks[...], hidden, across, preferred_element_type=F32)
    for p in range(nf):
        piece = seed_sums[p * 8 : p * 8 + 8]
        s3[p] = jnp.concatenate([piece[:, 0:LANES], piece[:, LANES:]], axis=0).astype(BF16)

    @pl.when(f == 0)
    def _():
        diagonal = lax.broadcasted_iota(jnp.int32, (LANES, LANES), 0) == lax.broadcasted_iota(
            jnp.int32, (LANES, LANES), 1
        )
        wide = lax.dot_general(
            jnp.where(diagonal, 1.0, 0.0).astype(BF16), hidden, across, preferred_element_type=F32
        )
        for p in range(nf):
            piece = wide[p * 8 : p * 8 + 8]
            hs[p] = jnp.concatenate([piece[:, 0:LANES], piece[:, LANES:]], axis=0).astype(BF16)

    def seeds_out(i):
        p = peer(i)
        send(s3.at[p], r3.at[f], fsem.at[2], fsem.at[3], at(ff=p))

        @pl.when(f == 0)
        def _():
            send(hs.at[p], rh, fsem.at[4], fsem.at[5], at(ff=p))

    loop(0, nf - 1, seeds_out)
    r3[f] = s3[f]

    @pl.when(f == 0)
    def _():
        rh[...] = hs[0]

    @pl.when(f != 0)
    def _():
        landed(rh, fsem.at[5])

    w2s = wall[:, 16:32, :].reshape(nf * 16, wall.shape[2])
    w2n = wall[:, 32:48, :].reshape(nf * 16, wall.shape[2])

    def rejoin(v):
        return jnp.concatenate([v[0:8], v[8:16]], axis=1).astype(BF16)

    logits = jnp.dot(rejoin(rh[...].astype(F32)), w2s, preferred_element_type=F32)
    landed(s3.at[pl.ds(0, nf - 1)], fsem.at[3])
    mean = jnp.zeros(r3.shape[1:], F32)
    for p in range(nf):
        mean += r3[p].astype(F32)
    logits += jnp.dot(rejoin(mean / FAN2), w2n, preferred_element_type=F32)

    s4[...] = logits
    other = at(ff=f + 1 - 2 * core)

    def along(i):
        yy = (y + order(i)) % (nf // 2)
        send(s4, r4.at[core, y], gsend.at[i], grecv.at[y], at(ff=yy * 2 + core))

    loop(0, nf // 2 - 1, along)
    send(s4, r4.at[core, y], gsend.at[nf // 2 - 1], psem.at[1, y], other)
    r4[core, y] = logits

    def onto(i):
        yy = (y + nf + (1 - 2 * (i % 2)) * (i // 2 + 1)) % (nf // 2)
        landed(s4, grecv.at[yy])
        send(r4.at[core, yy], r4.at[core, yy], psem.at[0, i], psem.at[1, yy], other)

    loop(0, nf // 2 - 1, onto)

    def sent(i):
        for kind, ref in ((0, a1), (1, b1), (2, bo), (3, ao), (4, ac), (5, bc)):
            landed(ref.at[i], xsend.at[kind, i])

    loop(0, NZ, sent)
    for i in range(NX - 1):
        landed(dgot.at[i], dsem.at[0, i])
    for i in range(NZ - 1):
        landed(zr.at[i], zsend.at[i])
        landed(dz_got.at[i], esem.at[0, i])
    landed(wall.at[pl.ds(0, nf - 1)], wsem.at[0])
    landed(near.at[pl.ds(0, nf - 1)], nsem.at[0, 0])
    landed(sums.at[pl.ds(0, nf - 1)], fsem.at[0])
    landed(s3.at[pl.ds(0, nf - 1)], fsem.at[2])

    @pl.when(f == 0)
    def _():
        landed(hs.at[pl.ds(0, nf - 1)], fsem.at[4])

    for i in range(nf // 2):
        landed(s4, gsend.at[i])
        landed(s4, psem.at[1, i])
    for i in range(nf // 2 - 1):
        landed(s4, psem.at[0, i])
    for i in range(nf):
        out[i] = r4[i % 2, i // 2]


def seed_logits(src, dst, rows, x, cols, xnear, w, nbrs, feats):
    self1, neigh1, self2, neigh2 = w
    hid = self1.shape[1]
    seeds = nbrs.shape[1]
    slots, depth = cols.shape[0] // (NX * NZ), cols.shape[1]
    body = feats * 8
    half = body // 2
    vm = pl.BlockSpec(memory_space=pltpu.VMEM)
    sm = pl.BlockSpec(memory_space=pltpu.SMEM)
    quarter = pltpu.VMEM((NZ, half, LANES), BF16)
    dma = pltpu.SemaphoreType.DMA
    return pl.pallas_call(
        step_kernel,
        out_shape=jax.ShapeDtypeStruct((feats, seeds // feats, hid), F32),
        in_specs=[sm] * 2 + [vm] * 3 + [pl.BlockSpec(memory_space=pl.ANY)] + [vm] * 6,
        out_specs=vm,
        scratch_shapes=[
            pltpu.VMEM((16, LANES), jnp.int32),
            pltpu.SMEM((16, LANES), jnp.int32),
            pltpu.VMEM((NX, NZ, LANES), F32),
            pltpu.VMEM((x.shape[1] // LANES, 8, LANES), F32),
            pltpu.VMEM((NX, NZ, slots, depth, LANES), jnp.int32),
            pltpu.VMEM((slots + 1, 8, LANES), F32),
            pltpu.VMEM((NX, NZ, body, LANES), BF16),
            pltpu.VMEM((48, hid), F32),
            pltpu.VMEM((48, hid), BF16),
            pltpu.VMEM((feats, 48, hid), BF16),
            *[quarter] * 8,
            pltpu.VMEM((NX - 1, NZ, LANES), F32),
            pltpu.VMEM((NZ, LANES), F32),
            pltpu.VMEM((NZ - 1, NZ, LANES), F32),
            pltpu.VMEM((NZ - 1, body, LANES), BF16),
            pltpu.VMEM((NZ - 1, body, LANES), BF16),
            pltpu.VMEM((seeds, LANES), BF16),
            pltpu.VMEM((hid, feats * 16), BF16),
            pltpu.VMEM((feats, 8, LANES), F32),
            pltpu.VMEM((feats, 8, LANES), F32),
            pltpu.VMEM((feats, 16, LANES), F32),
            pltpu.VMEM((feats, 16, LANES), BF16),
            pltpu.VMEM((feats, 16, LANES), BF16),
            pltpu.VMEM((feats, 16, LANES), BF16),
            pltpu.VMEM((16, LANES), BF16),
            pltpu.VMEM((8, hid), F32),
            pltpu.VMEM((2, feats // 2, 8, hid), F32),
            dma(()),
            dma((NZ,)),
            dma((2,)),
            dma((2, feats)),
            dma((6, NZ)),
            dma((6, NZ)),
            dma((2, NX - 1)),
            dma((2, NZ - 1)),
            dma((NZ - 1,)),
            dma((NZ - 1,)),
            dma((6,)),
            dma((feats // 2,)),
            dma((feats // 2,)),
            dma((2, feats // 2)),
        ],
        compiler_params=pltpu.CompilerParams(
            collective_id=0, has_side_effects=True, vmem_limit_bytes=VMEM
        ),
    )(
        src, rows, dst.reshape(8, LANES), rows.reshape(8, LANES), x,
        cols.reshape(NX, NZ, slots, depth, LANES), xnear, self1, neigh1, self2, neigh2, nbrs,
    )


def loss_kernel(table, labels, logits, loss):
    full = jnp.transpose(table[...])
    rows = full[0 : logits.shape[0]]
    logits[...] = rows
    classes = lax.broadcasted_iota(jnp.int32, rows.shape, 0)
    picked = jnp.sum(jnp.where(classes == labels[...], rows, 0.0), axis=0, keepdims=True)
    loss[...] = jnp.log(jnp.sum(jnp.exp(rows), axis=0, keepdims=True)) - picked


def per_device(
    x_far,
    x_near,
    tile_src,
    tile_dst,
    tile_rows,
    tile_cols,
    seed_nbrs,
    labels,
    self_one,
    neigh_one,
    self_two,
    neigh_two,
):
    feats = lax.axis_size("feat")
    classes, hid = self_two.shape[0], self_one.shape[0]
    seeds = labels.shape[0]
    weights = (self_one.T, neigh_one.T, self_two.T, neigh_two.T)
    table = seed_logits(
        tile_src, tile_dst, tile_rows, x_far, tile_cols, x_near, weights, seed_nbrs.T, feats
    )
    logits, loss = pl.pallas_call(
        loss_kernel,
        out_shape=(
            jax.ShapeDtypeStruct((classes, seeds), F32),
            jax.ShapeDtypeStruct((1, seeds), F32),
        ),
        compiler_params=pltpu.CompilerParams(vmem_limit_bytes=VMEM),
    )(table.reshape(seeds, hid), labels.reshape(1, seeds))
    return logits, loss.reshape(seeds)


def solution(mesh):
    placed = (
        P("feat", "node"),
        P("feat", "node"),
        P("node"),
        P("node"),
        P("node"),
        P("node", None, None),
        P("node", None),
        P("node"),
        P(None, "feat"),
        P(None, "feat"),
        P(None, "feat"),
        P(None, "feat"),
    )
    return jax.shard_map(
        per_device,
        mesh=mesh,
        in_specs=placed,
        out_specs=(P(None, "node"), P("node")),
        check_vma=False,
    )
```

```python
import functools

import jax
import jax.numpy as jnp
from jax import lax
from jax.experimental import pallas as pl
from jax.experimental.pallas import tpu as pltpu
from jax.sharding import PartitionSpec as P

FAN2 = 10
NX, NZ = 4, 8
LANES = 128
VMEM = 60 * 1024 * 1024
MESH = pl.DeviceIdType.MESH
F32, BF16 = jnp.float32, jnp.bfloat16


def slot_plan(d):
    slots = 32
    pos = lax.broadcasted_iota(jnp.int32, d.shape, 1) % slots
    prev = jnp.full(d.shape, slots, jnp.int32)
    for s in range(slots - 1, 0, -1):
        prev = jnp.where((pos >= s) & (pltpu.roll(d, s, 1) == d), pos - s, prev)
    last = jnp.full(d.shape, slots, jnp.int32)
    for b in range(16):
        v = jnp.where(d == b, pos, -1)
        for s in (1, 2, 4, 8, 16):
            v = jnp.maximum(v, jnp.where((pos & s) == 0, pltpu.roll(v, LANES - s, 1), pltpu.roll(v, s, 1)))
        last = jnp.where((pos == b) & (v >= 0), v, last)
    return prev, last


def block_counts(rows, degp):
    columns = jnp.transpose(jnp.concatenate([rows.astype(F32)] * 16, axis=0))
    across = lax.broadcasted_iota(jnp.int32, (LANES, LANES), 1).astype(F32)
    for r in range(8):
        live = jnp.where(across < columns[:, r : r + 1], 1.0, 0.0)
        sums = jnp.sum(live.reshape(4, LANES // 4, LANES), axis=1)
        degp[r // 2, (r % 2) * 4 : (r % 2) * 4 + 4, :] = sums


def step_kernel(
    src, rows, dst_v, rows_v, x_ref, cols, xnear, self1, neigh1, self2, neigh2, nbrs, out,
    plan_v, plan_s, degp, xs, cv, buf0, buf1, buf2, parts, stage, weights, wall, a1, b1, a2, b2, ac, ao, bo, bc, dgot, degx, dz_got,
    zs, zr, picks, w1t, near, sums, r2, s3, hs, r3, rh, s4, r4,
    plan_sem, csem, wsem, nsem, xsend, xrecv, dsem, esem, zsend, zrecv, fsem, gsend, grecv, psem,
):
    node, f = lax.axis_index("node"), lax.axis_index("feat")
    x, z = node // NZ, node % NZ
    y, core = f // 2, f % 2
    nf = wall.shape[0]
    xp, xm, xo = (x + 1) % NX, (x + NX - 1) % NX, (x + 2) % NX
    half = a1.shape[1]
    body = 2 * half
    slots, depth = cv.shape[2], cv.shape[3]

    def at(xx=x, zz=z, ff=f):
        return {"node": xx * NZ + zz, "feat": ff}

    def send(source, target, send_sem, recv_sem, device):
        copy = pltpu.make_async_remote_copy(
            src_ref=source, dst_ref=target, send_sem=send_sem, recv_sem=recv_sem,
            device_id=device, device_id_type=MESH,
        )
        copy.start()

    def landed(ref, sem):
        pltpu.make_async_copy(ref, ref, sem).wait()

    def order(i):
        return (4 + (1 - 2 * (i % 2)) * ((i + 1) // 2)) % NZ

    def peer(i):
        return (f + nf // 2 + (1 - 2 * (i % 2)) * ((i + 1) // 2)) % nf

    def loop(lo, hi, fn):
        lax.fori_loop(lo, hi, lambda i, c: (fn(i), c)[1], 0)

    barrier = pltpu.get_barrier_semaphore()

    def greet(device):
        pl.semaphore_signal(barrier, inc=1, device_id=device, device_id_type=MESH)

    loop(0, NX - 1, lambda i: greet(at(xx=(x + 1 + i) % NX)))
    loop(0, NZ - 1, lambda i: greet(at(zz=(z + 1 + i) % NZ)))
    loop(0, nf - 1, lambda i: greet(at(ff=(f + 1 + i) % nf)))

    def columns_in(i):
        zi = (z + order(i)) % NZ
        pltpu.make_async_copy(cols.at[:, zi], cv.at[:, zi], csem.at[i]).start()

    loop(0, NZ, columns_in)

    plan_v[0:8], plan_v[8:16] = slot_plan(dst_v[...])
    plan_copy = pltpu.make_async_copy(plan_v, plan_s, plan_sem)
    plan_copy.start()
    for b in range(xs.shape[0]):
        xs[b] = x_ref[:, b * LANES : (b + 1) * LANES].astype(F32)
    for buf in (buf0, buf1, buf2):
        buf[...] = jnp.zeros_like(buf)
    for b in range(nf):
        near[b] = xnear[:, b * LANES : (b + 1) * LANES].astype(F32)
    stage[...] = jnp.zeros_like(stage)
    stage[0:8] = self1[...].astype(F32)
    stage[8:16] = neigh1[...].astype(F32)
    stage[16:32, 0 : self2.shape[1]] = self2[...].astype(F32)
    stage[32:48, 0 : neigh2.shape[1]] = neigh2[...].astype(F32)
    weights[...] = stage[...].astype(BF16)
    lane = lax.broadcasted_iota(jnp.int32, (8, LANES), 1)

    rows_of = lax.broadcasted_iota(jnp.int32, (16, LANES), 0)
    ids = [(rows_of + 16 * g).astype(jnp.int16) for g in range(LANES // 16)]
    one, zero = jnp.ones((16, LANES), BF16), jnp.zeros((16, LANES), BF16)

    def gathered(block, xx, zi, s):
        got = []
        for k in range(depth):
            index = jnp.broadcast_to(cv[xx, zi, s, pl.ds(k, 1), :], (8, LANES))
            got.append(jnp.take_along_axis(block, index, axis=1, mode="promise_in_bounds"))
        return functools.reduce(lambda a, b: a + b, got)

    def counted(block, xx, zi, s):
        index = [
            jnp.broadcast_to(cv[xx, zi, s, pl.ds(k, 1), :], (16, LANES)).astype(jnp.int16)
            for k in range(depth)
        ]
        groups = []
        for g in ids:
            hits = [jnp.where(row == g, one, zero) for row in index]
            groups.append(functools.reduce(lambda a, b: a + b, hits))
        matrix = jnp.concatenate(groups, axis=0)
        return jnp.dot(block.astype(BF16), matrix, preferred_element_type=F32)

    def tile_sums(xx, zi, buf):
        target = xx * NZ + zi
        base, line, lane0 = target * slots, target // 4, target % 4 * slots
        for s in range(slots):
            block = xs[src[base + s]]
            total = (counted if s % 8 in (2, 5, 7) else gathered)(block, xx, zi, s)
            buf[s] = jnp.where(lane < rows[base + s], total, 0.0) + buf[plan_s[line, lane0 + s]]
        for b in range(0, nf, 2):
            pair = [buf[plan_s[8 + line, lane0 + b + j]] for j in (0, 1)]
            parts[xx, zi, b * 8 : b * 8 + 16] = jnp.concatenate(pair, axis=0).astype(BF16)

    def first(i):
        zi = (z + order(i)) % NZ
        send(parts.at[xo, zi, pl.ds(0, half)], a1.at[zi], xsend.at[0, zi], xrecv.at[0, zi], at(xx=xp))
        send(parts.at[xo, zi, pl.ds(half, half)], b1.at[zi], xsend.at[1, zi], xrecv.at[1, zi], at(xx=xm))

    def direct_up(i):
        zi = (z + order(i)) % NZ
        send(parts.at[xp, zi, pl.ds(half, half)], bo.at[zi], xsend.at[2, zi], xrecv.at[2, zi], at(xx=xp))

    def direct_down(i):
        zi = (z + order(i)) % NZ
        send(parts.at[xm, zi, pl.ds(0, half)], ao.at[zi], xsend.at[3, zi], xrecv.at[3, zi], at(xx=xm))

    def relay_up(i):
        zi = (z + order(i)) % NZ
        landed(a1.at[zi], xrecv.at[0, zi])
        a2[zi] = (a1[zi].astype(F32) + parts[xp, zi, pl.ds(0, half), :].astype(F32)).astype(BF16)
        send(a2.at[zi], ac.at[zi], xsend.at[4, zi], xrecv.at[4, zi], at(xx=xp))

    def relay_down(i):
        zi = (z + order(i)) % NZ
        landed(b1.at[zi], xrecv.at[1, zi])
        b2[zi] = (b1[zi].astype(F32) + parts[xm, zi, pl.ds(half, half), :].astype(F32)).astype(BF16)
        send(b2.at[zi], bc.at[zi], xsend.at[5, zi], xrecv.at[5, zi], at(xx=xm))

    def summed(i):
        zi = (z + order(i)) % NZ
        for kind, ref in ((2, bo), (3, ao), (4, ac), (5, bc)):
            landed(ref.at[zi], xrecv.at[kind, zi])
        upper = parts[x, zi, pl.ds(0, half), :].astype(F32) + ao[zi].astype(F32) + ac[zi].astype(F32)
        lower = parts[x, zi, pl.ds(half, half), :].astype(F32) + bo[zi].astype(F32) + bc[zi].astype(F32)
        return upper, lower

    def onward(i):
        dz = order(i)
        zi = (z + dz) % NZ
        upper, lower = summed(i)
        zs[dz - 1, 0:half] = upper.astype(BF16)
        zs[dz - 1, half:body] = lower.astype(BF16)
        send(zs.at[dz - 1], zr.at[dz - 1], zsend.at[dz - 1], zrecv.at[dz - 1], at(zz=zi))

    plan_copy.wait()

    wall[f] = weights[...]
    r2[f, 0:8] = near[f]

    def early(i):
        p = peer(i)
        send(near.at[p], r2.at[f, pl.ds(0, 8)], nsem.at[0, 0], nsem.at[1, f], at(ff=p))
        send(weights, wall.at[f], wsem.at[0], wsem.at[1], at(ff=p))

    def far(j):
        for i in (2 * j, 2 * j + 1):
            landed(cv.at[:, 0], csem.at[i])
        tile_sums(xo, (z + order(2 * j)) % NZ, buf0)
        tile_sums(xo, (z + order(2 * j + 1)) % NZ, buf1)

    def far_out(j):
        far(j)
        first(2 * j)
        first(2 * j + 1)

    far(0)
    pl.semaphore_wait(barrier, NX - 1 + NZ - 1 + nf - 1)
    loop(0, 2, first)
    loop(1, NZ // 2, far_out)
    onward_lag = 3

    def beside(i):
        zi = (z + order(i)) % NZ
        early(i)
        tile_sums(xp, zi, buf0)
        tile_sums(xm, zi, buf1)
        direct_up(i)
        direct_down(i)
        relay_up(i)
        relay_down(i)
        tile_sums(x, zi, buf2)

        @pl.when(i < nf - 1 - NZ)
        def _():
            early(NZ + i)

        @pl.when(i >= onward_lag)
        def _():
            onward(i - onward_lag)

    loop(0, NZ, beside)

    block_counts(jnp.where(dst_v[...] == f, rows_v[...], 0), degp)
    for i in range(NX - 1):
        send(degp.at[(x + 1 + i) % NX], dgot.at[i], dsem.at[0, i], dsem.at[1, i], at(xx=(x + 1 + i) % NX))
    loop(NZ - onward_lag, NZ - 1, onward)
    for i in range(NX - 1):
        landed(dgot.at[i], dsem.at[1, i])
    degx[...] = degp[x] + dgot[0] + dgot[1] + dgot[2]
    for dz in range(1, NZ):
        send(degx, dz_got.at[dz - 1], esem.at[0, dz - 1], esem.at[1, dz - 1], at(zz=(z + dz) % NZ))

    own_nodes = lax.broadcasted_iota(jnp.int32, (LANES, nbrs.shape[1]), 0) + f * LANES
    counts = jnp.zeros(own_nodes.shape, F32)
    for n in range(FAN2):
        counts += jnp.where(nbrs[n : n + 1, :] == own_nodes, 1.0, 0.0)
    picks[...] = jnp.transpose(counts).astype(BF16)
    landed(wall.at[pl.ds(0, nf - 1)], wsem.at[1])
    w1 = wall[:, 0:16, :].reshape(nf * 16, wall.shape[2])
    w1t[...] = jnp.transpose(w1.astype(F32)).astype(BF16)

    upper, lower = summed(NZ - 1)
    for i in (3, 2, 4, 1, 5, 0, 6):
        landed(zr.at[i], zrecv.at[i])
        upper += zr[i, 0:half].astype(F32)
        lower += zr[i, half:body].astype(F32)
    for b in range(nf // 2):
        sums[b] = upper[b * 8 : b * 8 + 8]
        sums[b + nf // 2] = lower[b * 8 : b * 8 + 8]

    def spread(i):
        p = peer(i)
        send(sums.at[p], r2.at[f, pl.ds(8, 8)], fsem.at[0], fsem.at[1], at(ff=p))

    loop(0, nf - 1, spread)
    r2[f, 8:16] = sums[f]
    deg = degx[pl.ds(z, 1), :]
    for i in range(NZ - 1):
        landed(dz_got.at[i], esem.at[1, i])
        deg += dz_got[i, pl.ds(z, 1), :]
    scale = 1.0 / jnp.maximum(4.0 * deg, 1.0)

    def near_in(i):
        p = (f + 1 + i) % nf
        landed(near.at[p], nsem.at[1, p])

    loop(0, nf - 1, near_in)
    landed(sums.at[pl.ds(0, nf - 1)], fsem.at[1])
    both = r2[...].reshape(nf * 16, LANES)
    is_sum = lax.broadcasted_iota(jnp.int32, both.shape, 0) % 16 >= 8
    both = jnp.where(is_sum, both * scale, both).astype(BF16)
    hidden = jnp.maximum(jnp.dot(w1t[...], both, preferred_element_type=F32), 0.0).astype(BF16)
    across = (((1,), (1,)), ((), ()))
    seed_sums = lax.dot_general(picks[...], hidden, across, preferred_element_type=F32)
    for p in range(nf):
        piece = seed_sums[p * 8 : p * 8 + 8]
        s3[p] = jnp.concatenate([piece[:, 0:LANES], piece[:, LANES:]], axis=0).astype(BF16)

    @pl.when(f == 0)
    def _():
        diagonal = lax.broadcasted_iota(jnp.int32, (LANES, LANES), 0) == lax.broadcasted_iota(
            jnp.int32, (LANES, LANES), 1
        )
        wide = lax.dot_general(
            jnp.where(diagonal, 1.0, 0.0).astype(BF16), hidden, across, preferred_element_type=F32
        )
        for p in range(nf):
            piece = wide[p * 8 : p * 8 + 8]
            hs[p] = jnp.concatenate([piece[:, 0:LANES], piece[:, LANES:]], axis=0).astype(BF16)

    def seeds_out(i):
        p = peer(i)
        send(s3.at[p], r3.at[f], fsem.at[2], fsem.at[3], at(ff=p))

        @pl.when(f == 0)
        def _():
            send(hs.at[p], rh, fsem.at[4], fsem.at[5], at(ff=p))

    loop(0, nf - 1, seeds_out)
    r3[f] = s3[f]

    @pl.when(f == 0)
    def _():
        rh[...] = hs[0]

    @pl.when(f != 0)
    def _():
        landed(rh, fsem.at[5])

    w2s = wall[:, 16:32, :].reshape(nf * 16, wall.shape[2])
    w2n = wall[:, 32:48, :].reshape(nf * 16, wall.shape[2])

    def rejoin(v):
        return jnp.concatenate([v[0:8], v[8:16]], axis=1).astype(BF16)

    logits = jnp.dot(rejoin(rh[...].astype(F32)), w2s, preferred_element_type=F32)
    landed(s3.at[pl.ds(0, nf - 1)], fsem.at[3])
    mean = jnp.zeros(r3.shape[1:], F32)
    for p in range(nf):
        mean += r3[p].astype(F32)
    logits += jnp.dot(rejoin(mean / FAN2), w2n, preferred_element_type=F32)

    s4[...] = logits
    other = at(ff=f + 1 - 2 * core)

    def along(i):
        yy = (y + order(i)) % (nf // 2)
        send(s4, r4.at[core, y], gsend.at[i], grecv.at[y], at(ff=yy * 2 + core))

    loop(0, nf // 2 - 1, along)
    send(s4, r4.at[core, y], gsend.at[nf // 2 - 1], psem.at[1, y], other)
    r4[core, y] = logits

    def onto(i):
        yy = (y + nf + (1 - 2 * (i % 2)) * (i // 2 + 1)) % (nf // 2)
        landed(s4, grecv.at[yy])
        send(r4.at[core, yy], r4.at[core, yy], psem.at[0, i], psem.at[1, yy], other)

    loop(0, nf // 2 - 1, onto)

    def sent(i):
        for kind, ref in ((0, a1), (1, b1), (2, bo), (3, ao), (4, ac), (5, bc)):
            landed(ref.at[i], xsend.at[kind, i])

    loop(0, NZ, sent)
    for i in range(NX - 1):
        landed(dgot.at[i], dsem.at[0, i])
    for i in range(NZ - 1):
        landed(zr.at[i], zsend.at[i])
        landed(dz_got.at[i], esem.at[0, i])
    landed(wall.at[pl.ds(0, nf - 1)], wsem.at[0])
    landed(near.at[pl.ds(0, nf - 1)], nsem.at[0, 0])
    landed(sums.at[pl.ds(0, nf - 1)], fsem.at[0])
    landed(s3.at[pl.ds(0, nf - 1)], fsem.at[2])

    @pl.when(f == 0)
    def _():
        landed(hs.at[pl.ds(0, nf - 1)], fsem.at[4])

    for i in range(nf // 2):
        landed(s4, gsend.at[i])
        landed(s4, psem.at[1, i])
    for i in range(nf // 2 - 1):
        landed(s4, psem.at[0, i])
    for i in range(nf):
        out[i] = r4[i % 2, i // 2]


def seed_logits(src, dst, rows, x, cols, xnear, w, nbrs, feats):
    self1, neigh1, self2, neigh2 = w
    hid = self1.shape[1]
    seeds = nbrs.shape[1]
    slots, depth = cols.shape[0] // (NX * NZ), cols.shape[1]
    body = feats * 8
    half = body // 2
    vm = pl.BlockSpec(memory_space=pltpu.VMEM)
    sm = pl.BlockSpec(memory_space=pltpu.SMEM)
    quarter = pltpu.VMEM((NZ, half, LANES), BF16)
    dma = pltpu.SemaphoreType.DMA
    return pl.pallas_call(
        step_kernel,
        out_shape=jax.ShapeDtypeStruct((feats, seeds // feats, hid), F32),
        in_specs=[sm] * 2 + [vm] * 3 + [pl.BlockSpec(memory_space=pl.ANY)] + [vm] * 6,
        out_specs=vm,
        scratch_shapes=[
            pltpu.VMEM((16, LANES), jnp.int32),
            pltpu.SMEM((16, LANES), jnp.int32),
            pltpu.VMEM((NX, NZ, LANES), F32),
            pltpu.VMEM((x.shape[1] // LANES, 8, LANES), F32),
            pltpu.VMEM((NX, NZ, slots, depth, LANES), jnp.int32),
            *[pltpu.VMEM((slots + 1, 8, LANES), F32)] * 3,
            pltpu.VMEM((NX, NZ, body, LANES), BF16),
            pltpu.VMEM((48, hid), F32),
            pltpu.VMEM((48, hid), BF16),
            pltpu.VMEM((feats, 48, hid), BF16),
            *[quarter] * 8,
            pltpu.VMEM((NX - 1, NZ, LANES), F32),
            pltpu.VMEM((NZ, LANES), F32),
            pltpu.VMEM((NZ - 1, NZ, LANES), F32),
            pltpu.VMEM((NZ - 1, body, LANES), BF16),
            pltpu.VMEM((NZ - 1, body, LANES), BF16),
            pltpu.VMEM((seeds, LANES), BF16),
            pltpu.VMEM((hid, feats * 16), BF16),
            pltpu.VMEM((feats, 8, LANES), F32),
            pltpu.VMEM((feats, 8, LANES), F32),
            pltpu.VMEM((feats, 16, LANES), F32),
            pltpu.VMEM((feats, 16, LANES), BF16),
            pltpu.VMEM((feats, 16, LANES), BF16),
            pltpu.VMEM((feats, 16, LANES), BF16),
            pltpu.VMEM((16, LANES), BF16),
            pltpu.VMEM((8, hid), F32),
            pltpu.VMEM((2, feats // 2, 8, hid), F32),
            dma(()),
            dma((NZ,)),
            dma((2,)),
            dma((2, feats)),
            dma((6, NZ)),
            dma((6, NZ)),
            dma((2, NX - 1)),
            dma((2, NZ - 1)),
            dma((NZ - 1,)),
            dma((NZ - 1,)),
            dma((6,)),
            dma((feats // 2,)),
            dma((feats // 2,)),
            dma((2, feats // 2)),
        ],
        compiler_params=pltpu.CompilerParams(
            collective_id=0, has_side_effects=True, vmem_limit_bytes=VMEM
        ),
    )(
        src, rows, dst.reshape(8, LANES), rows.reshape(8, LANES), x,
        cols.reshape(NX, NZ, slots, depth, LANES), xnear, self1, neigh1, self2, neigh2, nbrs,
    )


def loss_kernel(table, labels, logits, loss):
    full = jnp.transpose(table[...])
    rows = full[0 : logits.shape[0]]
    logits[...] = rows
    classes = lax.broadcasted_iota(jnp.int32, rows.shape, 0)
    picked = jnp.sum(jnp.where(classes == labels[...], rows, 0.0), axis=0, keepdims=True)
    loss[...] = jnp.log(jnp.sum(jnp.exp(rows), axis=0, keepdims=True)) - picked


def per_device(
    x_far,
    x_near,
    tile_src,
    tile_dst,
    tile_rows,
    tile_cols,
    seed_nbrs,
    labels,
    self_one,
    neigh_one,
    self_two,
    neigh_two,
):
    feats = lax.axis_size("feat")
    classes, hid = self_two.shape[0], self_one.shape[0]
    seeds = labels.shape[0]
    weights = (self_one.T, neigh_one.T, self_two.T, neigh_two.T)
    table = seed_logits(
        tile_src, tile_dst, tile_rows, x_far, tile_cols, x_near, weights, seed_nbrs.T, feats
    )
    logits, loss = pl.pallas_call(
        loss_kernel,
        out_shape=(
            jax.ShapeDtypeStruct((classes, seeds), F32),
            jax.ShapeDtypeStruct((1, seeds), F32),
        ),
        compiler_params=pltpu.CompilerParams(vmem_limit_bytes=VMEM),
    )(table.reshape(seeds, hid), labels.reshape(1, seeds))
    return logits, loss.reshape(seeds)


def solution(mesh):
    placed = (
        P("feat", "node"),
        P("feat", "node"),
        P("node"),
        P("node"),
        P("node"),
        P("node", None, None),
        P("node", None),
        P("node"),
        P(None, "feat"),
        P(None, "feat"),
        P(None, "feat"),
        P(None, "feat"),
    )
    return jax.shard_map(
        per_device,
        mesh=mesh,
        in_specs=placed,
        out_specs=(P(None, "node"), P("node")),
        check_vma=False,
    )
```
